128 devices in a mesh: band: 32 (over y_hi, x, z), grid: 4 (over y_lo, core).
Axes of the slice: x: 4, y: 4 (y_hi: 2, y_lo: 2; y = y_hi * 2 + y_lo), z: 4, core: 2. Of those that a mesh axis runs over, the one named last changes fastest.
Arguments:
- orbitals: float32 [64, 128, 16384], P('band', 'grid'), may hold values from -6 to 6
- occupation: float32 [64], P('band'), may hold values from 0.1 to 1
- pair_keep: int32 [64, 2, 2], P('band'), may hold values 0 or 1
Outputs:
- exchange_term: float32 [64, 128, 16384], P('band', 'grid')
The draws below stay inside these ranges and needn't reach their ends.
All inputs are finite; a program needn't handle non-finite values. No bound on the sum of `pair_keep` on one device may be relied on, other than what follows from the above.
Results may differ from the reference program's by a relative error of at most 0.0065.
Values may be sent and summed in bfloat16 or wider, within the bound.
A program may use at most 128 MiB of HBM per device.

```python
import math
import jax
import jax.numpy as jnp
from jax import lax

GRID = 128
BANDS_DEV = 2
BANDS = 64
N_BAND = 32


def plant(array, stream_key, low, top_value):
    longest = array.shape.index(max(array.shape))
    spots = []
    for shift in (0, 1):
        where = [jax.random.randint(jax.random.fold_in(stream_key, axis), (), 0, length) for axis, length in enumerate(array.shape)]
        where[longest] = (where[longest] + shift) % array.shape[longest]
        spots.append(tuple(where))
    return array.at[spots[0]].set(low).at[spots[1]].set(top_value)


def shard_levels(key, extent, shards, low, largest):
    level, own = 1.0, jax.random.fold_in(key, 6)
    for dim, shards_of in shards:
        steps = jnp.exp(jax.random.uniform(jax.random.fold_in(own, dim), (shards_of,), jnp.float32, low / len(shards), largest / len(shards)))
        level = level * jnp.repeat(steps, extent[dim] // shards_of).reshape([-1 if axis == dim else 1 for axis in range(len(extent))])
    return level


def centred(rng, extent, width, reach, split=(), kind=jnp.bfloat16):
    values = width * jax.random.normal(rng, extent, jnp.float32)
    if split:
        values = values * shard_levels(rng, extent, split, -0.22, 0.18)
    return jnp.clip(values, -reach, reach).astype(kind)


def setup_inputs(seed: int = 0) -> dict:
    splits = jax.random.split(jax.random.key(seed), 4)
    orbitals = centred(splits[0], (BANDS, GRID, GRID * GRID), 1.0, 6.0, ((0, 32), (1, 4)), jnp.float32)
    occupation = jnp.clip(0.1 + 0.9 * jax.random.uniform(splits[1], (BANDS,), jnp.float32) ** shard_levels(splits[1], (BANDS,), ((0, 32),), -0.2, 0.2), 0.1, 1.0)
    pair_keep = plant((jax.random.randint(splits[2], (BANDS, 2, BANDS_DEV), 0, 4) < 3).astype(jnp.int32), jax.random.fold_in(splits[2], 1), 0, 1)
    return dict(orbitals=orbitals, occupation=occupation, pair_keep=pair_keep)


screen_width = 64.0


def make_tables():
    wave_index = jnp.arange(GRID, dtype=jnp.int32)
    phase_angle = ((wave_index[:, None] * wave_index[None, :]) % GRID).astype(jnp.float32) * (2.0 * math.pi / GRID)
    cosine = jnp.cos(phase_angle)
    sine_part = jnp.sin(phase_angle)
    result_tables = []
    for direction_sign in (1.0, -1.0):
        signed_sine = sine_part * direction_sign
        line_table = jnp.concatenate([cosine, signed_sine], axis=1).astype(jnp.bfloat16)
        square_table = jnp.concatenate([jnp.concatenate([cosine, -signed_sine], axis=1), jnp.concatenate([signed_sine, cosine], axis=1)], axis=0).astype(jnp.bfloat16)
        result_tables.append((line_table, square_table))
    return result_tables


def signed_freq(indices):
    return jnp.where(indices >= GRID // 2, indices - GRID, indices).astype(jnp.float32)


def coulomb_kernel(rows_x, rows_y):
    depth_index = jnp.arange(2 * GRID, dtype=jnp.int32) % GRID
    squared = signed_freq(rows_x)[:, None, None] ** 2 + signed_freq(rows_y)[None, :, None] ** 2 + signed_freq(depth_index)[None, None, :] ** 2
    scaled_q = squared / screen_width
    safe_q = jnp.where(scaled_q > 0, scaled_q, 1.0)
    ratio = jnp.where(scaled_q > 0, -jnp.expm1(-scaled_q) / safe_q, 1.0)
    return ratio * (4.0 / GRID ** 3)


def rotated(values):
    half_width = values.shape[-1] // 2
    return jnp.concatenate([values[..., half_width:], -values[..., :half_width]], axis=-1)


def along_y(table, values):
    stacked = jnp.concatenate([values, rotated(values)], axis=2).astype(jnp.float32)
    return jnp.einsum("vy,nxyk->nxvk", table.astype(jnp.float32), stacked)


def along_x(table, values):
    stacked = jnp.concatenate([values, rotated(values)], axis=1).astype(jnp.float32)
    return jnp.einsum("vx,nxyk->nvyk", table.astype(jnp.float32), stacked)


def pair_terms(own_bands, own_occ, visit_pairs, visit_occ, keep_rows, tables, kernel):
    group = own_bands.shape[0]
    halves = visit_pairs.shape[0]
    plane_rows = own_bands.shape[1]
    forward_tables, inverse_tables = tables
    own_grid = own_bands.reshape(group, plane_rows, GRID, GRID)
    own_twice = jnp.concatenate([own_grid, own_grid], axis=-1)
    density = (own_twice[:, None] * visit_pairs[None]).reshape(group * halves, plane_rows, GRID, 2 * GRID).astype(jnp.bfloat16)
    spectrum = jnp.dot(density.astype(jnp.float32), forward_tables[1].astype(jnp.float32)).astype(jnp.bfloat16)
    spectrum = along_y(forward_tables[0], spectrum).astype(jnp.bfloat16)
    screened = (along_x(forward_tables[0], spectrum) * kernel).astype(jnp.bfloat16)
    spectrum = along_x(inverse_tables[0], screened).astype(jnp.bfloat16)
    spectrum = along_y(inverse_tables[0], spectrum).astype(jnp.bfloat16)
    potential = jnp.dot(spectrum.astype(jnp.float32), inverse_tables[1].astype(jnp.float32))
    potential = potential.reshape(group, halves, plane_rows, GRID, 2 * GRID)
    keep_float = keep_rows.astype(jnp.float32)
    weight_own = jnp.repeat((visit_occ[None, :] * keep_float).reshape(group, halves, 2), GRID, axis=-1)
    weight_partner = jnp.repeat((own_occ[:, None] * keep_float).reshape(group, halves, 2), GRID, axis=-1)
    own_sum = jnp.sum(weight_own[:, :, None, None, :] * potential * visit_pairs[None], axis=1)
    own_part = (own_sum[..., :GRID] + own_sum[..., GRID:]).reshape(group, plane_rows, GRID * GRID)
    partner_sum = jnp.sum(weight_partner[:, :, None, None, :] * potential * own_twice[:, None], axis=0)
    partner_part = partner_sum.reshape(halves, plane_rows, GRID, 2, GRID).transpose(0, 3, 1, 2, 4).reshape(2 * halves, plane_rows, GRID * GRID)
    return own_part, partner_part


def reference(orbitals, occupation, pair_keep):
    tables = make_tables()
    full_index = jnp.arange(GRID, dtype=jnp.int32)
    kernel = coulomb_kernel(full_index, full_index)
    band_blocks = orbitals.reshape(N_BAND, BANDS_DEV, GRID, GRID * GRID)
    occ_blocks = occupation.reshape(N_BAND, BANDS_DEV)
    keep_blocks = pair_keep.reshape(N_BAND, BANDS_DEV, 2, BANDS_DEV)
    halves = BANDS_DEV // 2

    def one_block(block_index):
        own_bands = band_blocks[block_index]
        own_occ = occ_blocks[block_index]
        results = []
        for offset in (1, 2):
            source = ((block_index - offset) % N_BAND).astype(jnp.int32)
            visitors = band_blocks[source]
            visit_pairs = visitors.reshape(halves, 2, GRID, GRID, GRID).transpose(0, 2, 3, 1, 4).reshape(halves, GRID, GRID, 2 * GRID)
            results.append(pair_terms(own_bands, own_occ, visit_pairs, occ_blocks[source], keep_blocks[block_index][:, offset - 1, :], tables, kernel))
        return results[0][0] + results[1][0], results[0][1], results[1][1]

    own_total, near_partner, far_partner = lax.map(one_block, jnp.arange(N_BAND, dtype=jnp.int32))
    total = own_total + jnp.roll(near_partner, -1, axis=0) + jnp.roll(far_partner, -2, axis=0)
    return (-total).reshape(BANDS, GRID, GRID * GRID)
```

```python
import functools
import math

import jax
import jax.numpy as jnp
from jax import lax
from jax.experimental import pallas as pl
from jax.experimental.pallas import tpu as pltpu
from jax.sharding import PartitionSpec as P

GRID = 128
WIDTH = 64.0
NCHUNK = 1
GROUP = 8
AXES = ("band", "grid")
BF = jnp.bfloat16
F32 = jnp.float32


def slot_order(g):
    chip, k = g // 2, g % 2
    return (2 + k, 3 - k, 1 - k, k) if chip == 0 else (k, 1 - k, 3 - k, 2 + k)


def routes(count):
    def pairs(to):
        out = []
        for c in range(count):
            for g in range(4):
                dc, dg = to(g // 2, g % 2)
                out.append((c * 4 + g, ((c + dc) % count) * 4 + dg))
        return out

    first = [
        pairs(lambda chip, k: (-1, 2 + k) if chip == 0 else (0, k)),
        pairs(lambda chip, k: (-1, 3 - k) if chip == 0 else (0, 1 - k)),
        pairs(lambda chip, k: (0, 1 - k) if chip == 0 else (-1, 3 - k)),
        pairs(lambda chip, k: (0, k) if chip == 0 else (-1, 2 + k)),
    ]
    second = [
        pairs(lambda chip, k: (1, 2 * chip + k)),
        pairs(lambda chip, k: (1, 2 * (1 - chip) + k)),
    ]
    core = pairs(lambda chip, k: (0, 2 * chip + 1 - k))
    return first, second, core


def back(pairs):
    return [(d, s) for s, d in pairs]


def send(value, pairs):
    return lax.ppermute(value, AXES, pairs)


def tables():
    index = jnp.arange(GRID, dtype=jnp.int32)
    angle = (index[:, None] * index[None, :] % GRID).astype(F32) * (2.0 * math.pi / GRID)
    cosine, sine = jnp.cos(angle), jnp.sin(angle)
    forward = jnp.concatenate(
        [jnp.concatenate([cosine, -sine], 1), jnp.concatenate([sine, cosine], 1)], 0
    ).astype(BF)
    inverse = jnp.concatenate(
        [jnp.concatenate([cosine, sine], 1), jnp.concatenate([-sine, cosine], 1)], 0
    ).astype(BF)
    return forward, inverse


def screened_kernel():
    index = jnp.arange(GRID, dtype=jnp.int32)
    freq = jnp.where(index >= GRID // 2, index - GRID, index).astype(F32)
    squared = freq[:, None, None] ** 2 + freq[None, :, None] ** 2 + freq[None, None, :] ** 2
    q = squared / WIDTH
    safe = jnp.where(q > 0, q, 1.0)
    ratio = jnp.where(q > 0, -jnp.expm1(-q) / safe, 1.0)
    return ratio * (4.0 / GRID**3)


def dot(left, right):
    return jnp.dot(left, right, preferred_element_type=F32)


def rows_of(parts, lanes, lead=None):
    if lead is None:
        return jnp.concatenate([p[:, lanes] for p in parts], 0)
    return jnp.concatenate([p[lead, :, lanes] for p in parts], 0)


def regroup(value):
    n = GRID
    top = jnp.concatenate([value[:n, :n], value[n:, :n]], 1)
    low = jnp.concatenate([value[:n, n:], value[n:, n:]], 1)
    return jnp.concatenate([top, low], 0)


def forward_body(tx, tz, a0, a1, a2, a3, b0, b1, b2, b3, *w):
    firsts, seconds = (a0, a1, a2, a3), (b0, b1, b2, b3)
    for pair in range(GROUP // 2):
        columns = []
        for half in range(2):
            at = (2 * pair + half) * GRID
            lanes = slice(at, at + GRID)
            own = rows_of(firsts, lanes)
            real = own * rows_of(seconds, lanes, 0)
            imag = own * rows_of(seconds, lanes, 1)
            columns.append(jnp.concatenate([real, imag], 0))
        packed = jnp.concatenate(columns, 1)
        mixed = regroup(dot(tx[...], packed).astype(BF))
        result = dot(mixed, tz[...])
        for half in range(2):
            for i in range(2):
                w[i][2 * pair + half] = result[half * GRID : (half + 1) * GRID, i * GRID : (i + 1) * GRID]


def middle_body(tf, ti, kern, *refs):
    count = 2 * NCHUNK
    parts, outs = (
        [r.reshape(r.shape[0] * 8, GRID) for r in refs[i : i + count]] for i in (0, count)
    )
    rows = GRID // NCHUNK
    for pair in range(4):
        columns = []
        for half in range(2):
            r = 2 * pair + half
            take = [f[pl.ds(r, rows, stride=8), :] for f in parts]
            columns.append(jnp.concatenate(take[0::2] + take[1::2], 0))
        packed = jnp.concatenate(columns, 1).astype(BF)
        spectrum = dot(tf[...], packed)
        factor = jnp.concatenate([kern[2 * pair], kern[2 * pair + 1]], 1)
        factor = jnp.concatenate([factor, factor], 0)
        field = (spectrum * factor).astype(BF)
        result = dot(ti[...], field)
        for half in range(2):
            r = 2 * pair + half
            for i, f in enumerate(outs):
                at = (i % 2) * GRID + (i // 2) * rows
                f[pl.ds(r, rows, stride=8), :] = result[
                    at : at + rows, half * GRID : (half + 1) * GRID
                ]


def inverse_body(weights, tx, tz, u0, u1, a0, a1, a2, a3, b0, b1, b2, b3, *outs):
    firsts, seconds = (a0, a1, a2, a3), (b0, b1, b2, b3)
    own_out, partner_out = outs[:4], outs[4:]
    wo0, wo1, wp0, wp1 = (weights[i] for i in range(4))
    for pair in range(GROUP // 2):
        packed = jnp.concatenate(
            [jnp.concatenate([u[2 * pair], u[2 * pair + 1]], 1) for u in (u0, u1)], 0
        ).astype(BF)
        mixed = regroup(dot(tx[...], packed).astype(BF))
        potential = dot(mixed, tz[...])
        for half in range(2):
            at = (2 * pair + half) * GRID
            lanes = slice(at, at + GRID)
            v0 = potential[half * GRID : (half + 1) * GRID, :GRID]
            v1 = potential[half * GRID : (half + 1) * GRID, GRID:]
            for i in range(4):
                rows = slice(32 * i, 32 * i + 32)
                x0, x1 = v0[rows], v1[rows]
                a = firsts[i][:, lanes].astype(F32)
                p0 = seconds[i][0, :, lanes].astype(F32)
                p1 = seconds[i][1, :, lanes].astype(F32)
                own_out[i][:, lanes] = ((wo0 * x0) * p0 + (wo1 * x1) * p1).astype(BF)
                partner_out[i][0, :, lanes] = ((wp0 * x0) * a).astype(BF)
                partner_out[i][1, :, lanes] = ((wp1 * x1) * a).astype(BF)


def whole(shape):
    return pl.BlockSpec(shape, lambda i: (0,) * len(shape))


def params():
    return pltpu.CompilerParams(
        dimension_semantics=("arbitrary",), vmem_limit_bytes=48 * 1024 * 1024
    )


def forward_call(tx, tz, firsts, seconds):
    lanes = firsts[0].shape[-1]
    ys = lanes // GRID
    step = GROUP * GRID
    return pl.pallas_call(
        forward_body,
        grid=(ys // GROUP,),
        in_specs=[whole((256, 256))] * 2
        + [pl.BlockSpec((32, step), lambda i: (0, i))] * 4
        + [pl.BlockSpec((2, 32, step), lambda i: (0, 0, i))] * 4,
        out_specs=[pl.BlockSpec((GROUP, GRID, GRID), lambda i: (i, 0, 0))] * 2,
        out_shape=[jax.ShapeDtypeStruct((ys, GRID, GRID), F32)] * 2,
        compiler_params=params(),
        name="forward",
    )(tx, tz, *firsts, *seconds)


def middle_call(tf, ti, kern, parts):
    ys = parts[0].shape[0]
    spec = pl.BlockSpec((ys, 8, GRID), lambda i: (0, i, 0))
    return pl.pallas_call(
        middle_body,
        grid=(GRID // 8,),
        in_specs=[whole((256, 256))] * 2
        + [pl.BlockSpec((8, GRID, GRID), lambda i: (i, 0, 0))]
        + [spec] * (2 * NCHUNK),
        out_specs=[spec] * (2 * NCHUNK),
        out_shape=[jax.ShapeDtypeStruct((ys, GRID, GRID), F32)] * (2 * NCHUNK),
        compiler_params=params(),
        name="middle",
    )(tf, ti, kern, *parts)


def inverse_call(weights, tx, tz, u, firsts, seconds):
    lanes = firsts[0].shape[-1]
    step = GROUP * GRID
    one = pl.BlockSpec((32, step), lambda i: (0, i))
    two = pl.BlockSpec((2, 32, step), lambda i: (0, 0, i))
    outs = pl.pallas_call(
        inverse_body,
        grid=(lanes // step,),
        in_specs=[pl.BlockSpec(memory_space=pltpu.SMEM)]
        + [whole((256, 256))] * 2
        + [pl.BlockSpec((GROUP, GRID, GRID), lambda i: (i, 0, 0))] * 2
        + [one] * 4
        + [two] * 4,
        out_specs=[one] * 4 + [two] * 4,
        out_shape=[jax.ShapeDtypeStruct((32, lanes), BF)] * 4
        + [jax.ShapeDtypeStruct((2, 32, lanes), BF)] * 4,
        compiler_params=params(),
        name="inverse",
    )(weights, tx, tz, *u, *firsts, *seconds)
    return outs[:4], outs[4:]


def body(orbitals, occupation, pair_keep):
    count = lax.axis_size("band")
    first_routes, second_routes, core_route = routes(count)
    c, g = lax.axis_index("band"), lax.axis_index("grid")
    chip, k = g // 2, g % 2

    small = jnp.concatenate(
        [occupation[:, None], pair_keep.reshape(2, 4).astype(F32)], 1
    )
    small = lax.all_gather(small, "band")
    lead = small[(c + chip) % count, k]
    partner_occ = small[(c + count - 1) % count, :, 0]
    keep = lax.dynamic_slice(lead, (1 + 2 * chip,), (2,))
    weights = -jnp.concatenate([partner_occ * keep, lead[0] * keep])

    table, table_inv = tables()
    order = jnp.asarray([slot_order(i) for i in range(4)], jnp.int32)[g]
    xs = (order[:, None] * 32 + jnp.arange(32, dtype=jnp.int32)[None]).reshape(-1)
    both = jnp.concatenate([xs, xs + GRID])
    left, left_inv = table.T, table_inv.T
    tx = left[:, both]
    tx_inv = left_inv[both, :]
    kern = screened_kernel()

    lanes = GRID * GRID // NCHUNK
    mine = orbitals.astype(BF)
    firsts, seconds, parts = [], [], []
    for n in range(NCHUNK):
        piece = mine[:, :, n * lanes : (n + 1) * lanes]
        same = lax.dynamic_index_in_dim(piece, k, 0, keepdims=False)
        other = lax.dynamic_index_in_dim(piece, 1 - k, 0, keepdims=False)
        f = [
            send(v, r) for v, r in zip((same, other, other, same), first_routes)
        ]
        s1, s2 = (send(piece, r) for r in second_routes)
        x1, x2 = send(s1, core_route), send(s2, core_route)
        s = [s2, x2, x1, s1]
        firsts.append(f)
        seconds.append(s)
        parts += forward_call(tx, table, f, s)
    fields = middle_call(left, left_inv, kern, parts)
    sames, others = [], []
    for n in range(NCHUNK):
        own, partner = inverse_call(weights, tx_inv, table_inv, fields[2 * n : 2 * n + 2], firsts[n], seconds[n])
        r0, r1, r2, r3 = (send(v, back(r)) for v, r in zip(own, first_routes))
        y0 = send(partner[1], core_route)
        y3 = send(partner[2], core_route)
        sum0 = (partner[0].astype(F32) + y0.astype(F32)).astype(BF)
        sum3 = (partner[3].astype(F32) + y3.astype(F32)).astype(BF)
        p3 = send(sum3, back(second_routes[0])).astype(F32)
        p0 = send(sum0, back(second_routes[1])).astype(F32)
        total = p0 + p3
        same = r0.astype(F32) + r3.astype(F32)
        other = r1.astype(F32) + r2.astype(F32)
        sames.append(jnp.where(k == 0, same, other) + total[0])
        others.append(jnp.where(k == 0, other, same) + total[1])
    return jnp.stack(
        [jnp.concatenate(sames, -1), jnp.concatenate(others, -1)]
    )


def solution(mesh):
    in_specs = (P("band", "grid", None), P("band"), P("band", None, None))
    return jax.shard_map(
        body, mesh=mesh, in_specs=in_specs, out_specs=P("band", "grid", None), check_vma=False
    )
```

```python
import functools
import math

import jax
import jax.numpy as jnp
from jax import lax
from jax.experimental import pallas as pl
from jax.experimental.pallas import tpu as pltpu
from jax.sharding import PartitionSpec as P

GRID = 128
WIDTH = 64.0
NCHUNK = 1
GROUP = 8
AXES = ("band", "grid")
BF = jnp.bfloat16
F32 = jnp.float32


def routes(count):
    def pairs(to):
        out = []
        for c in range(count):
            for g in range(4):
                dc, dg = to(g // 2, g % 2)
                out.append((c * 4 + g, ((c + dc) % count) * 4 + dg))
        return out

    straight = pairs(lambda p, k: (-1, 2 * p) if k == 0 else (2, 2 * p + 1))
    crossed = pairs(lambda p, k: (2, 2 * p + 1) if k == 0 else (-1, 2 * p))
    chip = pairs(lambda p, k: (0, 2 * (1 - p) + k))
    core = pairs(lambda p, k: (0, 2 * p + 1 - k))
    return straight, crossed, chip, core


def back(pairs):
    return [(d, s) for s, d in pairs]


def send(value, pairs):
    return lax.ppermute(value, AXES, pairs)


def tables():
    index = jnp.arange(GRID, dtype=jnp.int32)
    angle = (index[:, None] * index[None, :] % GRID).astype(F32) * (2.0 * math.pi / GRID)
    cosine, sine = jnp.cos(angle), jnp.sin(angle)
    forward = jnp.concatenate(
        [jnp.concatenate([cosine, -sine], 1), jnp.concatenate([sine, cosine], 1)], 0
    ).astype(BF)
    inverse = jnp.concatenate(
        [jnp.concatenate([cosine, sine], 1), jnp.concatenate([-sine, cosine], 1)], 0
    ).astype(BF)
    return forward, inverse


def screened_kernel():
    index = jnp.arange(GRID, dtype=jnp.int32)
    freq = jnp.where(index >= GRID // 2, index - GRID, index).astype(F32)
    squared = freq[:, None, None] ** 2 + freq[None, :, None] ** 2 + freq[None, None, :] ** 2
    q = squared / WIDTH
    safe = jnp.where(q > 0, q, 1.0)
    ratio = jnp.where(q > 0, -jnp.expm1(-q) / safe, 1.0)
    return ratio * (4.0 / GRID**3)


def dot(left, right):
    return jnp.dot(left, right, preferred_element_type=F32)


def rows_of(parts, lanes, lead=None):
    if lead is None:
        return jnp.concatenate([p[:, lanes] for p in parts], 0)
    return jnp.concatenate([p[lead, :, lanes] for p in parts], 0)


def regroup(value):
    n = GRID
    top = jnp.concatenate([value[:n, :n], value[n:, :n]], 1)
    low = jnp.concatenate([value[:n, n:], value[n:, n:]], 1)
    return jnp.concatenate([top, low], 0)


def forward_body(tx, tz, a0, a1, a2, a3, b0, b1, b2, b3, *w):
    firsts, seconds = (a0, a1, a2, a3), (b0, b1, b2, b3)
    for pair in range(GROUP // 2):
        columns = []
        for half in range(2):
            at = (2 * pair + half) * GRID
            lanes = slice(at, at + GRID)
            own = rows_of(firsts, lanes)
            real = own * rows_of(seconds, lanes, 0)
            imag = own * rows_of(seconds, lanes, 1)
            columns.append(jnp.concatenate([real, imag], 0))
        packed = jnp.concatenate(columns, 1)
        mixed = regroup(dot(tx[...], packed).astype(BF))
        result = dot(mixed, tz[...])
        for half in range(2):
            for i in range(2):
                w[i][2 * pair + half] = result[half * GRID : (half + 1) * GRID, i * GRID : (i + 1) * GRID]


def middle_body(tf, ti, kern, *refs):
    count = 2 * NCHUNK
    parts, outs = (
        [r.reshape(r.shape[0] * 8, GRID) for r in refs[i : i + count]] for i in (0, count)
    )
    rows = GRID // NCHUNK
    for pair in range(4):
        columns = []
        for half in range(2):
            r = 2 * pair + half
            take = [f[pl.ds(r, rows, stride=8), :] for f in parts]
            columns.append(jnp.concatenate(take[0::2] + take[1::2], 0))
        packed = jnp.concatenate(columns, 1).astype(BF)
        spectrum = dot(tf[...], packed)
        factor = jnp.concatenate([kern[2 * pair], kern[2 * pair + 1]], 1)
        factor = jnp.concatenate([factor, factor], 0)
        field = (spectrum * factor).astype(BF)
        result = dot(ti[...], field)
        for half in range(2):
            r = 2 * pair + half
            for i, f in enumerate(outs):
                at = (i % 2) * GRID + (i // 2) * rows
                f[pl.ds(r, rows, stride=8), :] = result[
                    at : at + rows, half * GRID : (half + 1) * GRID
                ]


def inverse_body(weights, tx, tz, u0, u1, a0, a1, a2, a3, b0, b1, b2, b3, *outs):
    firsts, seconds = (a0, a1, a2, a3), (b0, b1, b2, b3)
    own_out, partner_out = outs[:4], outs[4:]
    wo0, wo1, wp0, wp1 = (weights[i] for i in range(4))
    for pair in range(GROUP // 2):
        packed = jnp.concatenate(
            [jnp.concatenate([u[2 * pair], u[2 * pair + 1]], 1) for u in (u0, u1)], 0
        ).astype(BF)
        mixed = regroup(dot(tx[...], packed).astype(BF))
        potential = dot(mixed, tz[...])
        for half in range(2):
            at = (2 * pair + half) * GRID
            lanes = slice(at, at + GRID)
            v0 = potential[half * GRID : (half + 1) * GRID, :GRID]
            v1 = potential[half * GRID : (half + 1) * GRID, GRID:]
            for i in range(4):
                rows = slice(32 * i, 32 * i + 32)
                x0, x1 = v0[rows], v1[rows]
                a = firsts[i][:, lanes].astype(F32)
                p0 = seconds[i][0, :, lanes].astype(F32)
                p1 = seconds[i][1, :, lanes].astype(F32)
                own_out[i][:, lanes] = ((wo0 * x0) * p0 + (wo1 * x1) * p1).astype(BF)
                partner_out[i][0, :, lanes] = ((wp0 * x0) * a).astype(BF)
                partner_out[i][1, :, lanes] = ((wp1 * x1) * a).astype(BF)


def whole(shape):
    return pl.BlockSpec(shape, lambda i: (0,) * len(shape))


def params():
    return pltpu.CompilerParams(
        dimension_semantics=("arbitrary",), vmem_limit_bytes=48 * 1024 * 1024
    )


def forward_call(tx, tz, firsts, seconds):
    lanes = firsts[0].shape[-1]
    ys = lanes // GRID
    step = GROUP * GRID
    return pl.pallas_call(
        forward_body,
        grid=(ys // GROUP,),
        in_specs=[whole((256, 256))] * 2
        + [pl.BlockSpec((32, step), lambda i: (0, i))] * 4
        + [pl.BlockSpec((2, 32, step), lambda i: (0, 0, i))] * 4,
        out_specs=[pl.BlockSpec((GROUP, GRID, GRID), lambda i: (i, 0, 0))] * 2,
        out_shape=[jax.ShapeDtypeStruct((ys, GRID, GRID), F32)] * 2,
        compiler_params=params(),
        name="forward",
    )(tx, tz, *firsts, *seconds)


def middle_call(tf, ti, kern, parts):
    ys = parts[0].shape[0]
    spec = pl.BlockSpec((ys, 8, GRID), lambda i: (0, i, 0))
    return pl.pallas_call(
        middle_body,
        grid=(GRID // 8,),
        in_specs=[whole((256, 256))] * 2
        + [pl.BlockSpec((8, GRID, GRID), lambda i: (i, 0, 0))]
        + [spec] * (2 * NCHUNK),
        out_specs=[spec] * (2 * NCHUNK),
        out_shape=[jax.ShapeDtypeStruct((ys, GRID, GRID), F32)] * (2 * NCHUNK),
        compiler_params=params(),
        name="middle",
    )(tf, ti, kern, *parts)


def inverse_call(weights, tx, tz, u, firsts, seconds):
    lanes = firsts[0].shape[-1]
    step = GROUP * GRID
    one = pl.BlockSpec((32, step), lambda i: (0, i))
    two = pl.BlockSpec((2, 32, step), lambda i: (0, 0, i))
    outs = pl.pallas_call(
        inverse_body,
        grid=(lanes // step,),
        in_specs=[pl.BlockSpec(memory_space=pltpu.SMEM)]
        + [whole((256, 256))] * 2
        + [pl.BlockSpec((GROUP, GRID, GRID), lambda i: (i, 0, 0))] * 2
        + [one] * 4
        + [two] * 4,
        out_specs=[one] * 4 + [two] * 4,
        out_shape=[jax.ShapeDtypeStruct((32, lanes), BF)] * 4
        + [jax.ShapeDtypeStruct((2, 32, lanes), BF)] * 4,
        compiler_params=params(),
        name="inverse",
    )(weights, tx, tz, *u, *firsts, *seconds)
    return outs[:4], outs[4:]


def body(orbitals, occupation, pair_keep):
    count = lax.axis_size("band")
    straight, crossed, chip_route, core_route = routes(count)
    g = lax.axis_index("grid")
    p, k = g // 2, g % 2

    small = jnp.concatenate(
        [occupation[:, None], pair_keep.reshape(2, 4).astype(F32)], 1
    )
    lead = lax.dynamic_index_in_dim(send(small, straight), p, 0, keepdims=False)
    far_keep = lax.dynamic_index_in_dim(small[:, 3:], p, 1, keepdims=False)
    keep = jnp.where(k == 0, lead[1:3], far_keep)
    weights = -jnp.concatenate([small[:, 0] * keep, lead[0] * keep])

    table, table_inv = tables()
    xs = ((g ^ jnp.arange(4))[:, None] * 32 + jnp.arange(32)[None]).reshape(-1)
    both = jnp.concatenate([xs, xs + GRID])
    left, left_inv = table.T, table_inv.T
    tx = left[:, both]
    tx_inv = left_inv[both, :]
    kern = screened_kernel()

    def pick(value, band):
        return lax.dynamic_index_in_dim(value, band, 0, keepdims=False)

    lanes = GRID * GRID // NCHUNK
    mine = orbitals.astype(BF)
    firsts, seconds, parts = [], [], []
    for n in range(NCHUNK):
        piece = mine[:, :, n * lanes : (n + 1) * lanes]
        away = send(piece, chip_route)
        f = [
            send(v, r)
            for v in (pick(piece, p), pick(away, p))
            for r in (straight, crossed)
        ]
        s = [piece, send(piece, core_route), away, send(away, core_route)]
        firsts.append(f)
        seconds.append(s)
        parts += forward_call(tx, table, f, s)
    fields = middle_call(left, left_inv, kern, parts)
    outs = []
    for n in range(NCHUNK):
        own, partner = inverse_call(
            weights, tx_inv, table_inv, fields[2 * n : 2 * n + 2], firsts[n], seconds[n]
        )
        r0, r1, r2, r3 = (
            send(v, back(r)).astype(F32) for v, r in zip(own, (straight, crossed) * 2)
        )
        sums = [
            partner[i].astype(F32) + send(partner[i + 1], core_route).astype(F32)
            for i in (0, 2)
        ]
        is_band = (jnp.arange(2) == p)[:, None, None]
        near = sums[0] + jnp.where(is_band, (r0 + r1)[None], 0.0)
        far = sums[1] + jnp.where(is_band, (r2 + r3)[None], 0.0)
        outs.append(near + send(far.astype(BF), chip_route).astype(F32))
    return jnp.concatenate(outs, -1)


def solution(mesh):
    in_specs = (P("band", "grid", None), P("band"), P("band", None, None))
    return jax.shard_map(
        body, mesh=mesh, in_specs=in_specs, out_specs=P("band", "grid", None), check_vma=False
    )
```

```python
import functools
import math

import jax
import jax.numpy as jnp
import numpy as np
from jax import lax
from jax.experimental import pallas as pl
from jax.experimental.pallas import tpu as pltpu
from jax.sharding import PartitionSpec as P

GRID = 128
SLAB = 32
BLOCKS = 32
HALF_RING = 16
WIDTH = 64.0
CHUNKS = 8
LANES = GRID * GRID // CHUNKS
PAIRS = LANES // (2 * GRID)
TILES = GRID // 8
BF = jnp.bfloat16
F32 = jnp.float32
MESH = pl.DeviceIdType.MESH


def tables():
    index = np.arange(GRID)
    angle = (index[:, None] * index[None, :] % GRID) * (2.0 * math.pi / GRID)
    cosine, sine = np.cos(angle), np.sin(angle)
    forward = np.block([[cosine, -sine], [sine, cosine]])
    return tuple(np.asarray(t, np.float32).astype(BF) for t in (forward, forward.T))


def dot(left, right):
    return jnp.dot(left, right, preferred_element_type=F32)


def regroup(value):
    n = GRID
    top = jnp.concatenate([value[:n, :n], value[n:, :n]], 1)
    low = jnp.concatenate([value[:n, n:], value[n:, n:]], 1)
    return jnp.concatenate([top, low], 0)


def kernel(
    occ, keep, orbitals, plus, minus, out,
    stage, lead, own, real, imag, factor, near_in, far_in, core_in, chip_in, note_out, note_in,
    load_sem, store_sem, send_a, recv_a, send_b, recv_b, note_sem,
):
    c, g = lax.axis_index("band"), lax.axis_index("grid")
    p, k = lax.div(g, 2), lax.rem(g, 2)
    spot = lax.rem(c, HALF_RING)
    odd = lax.rem(c, 2)

    def block(step):
        return lax.rem(c + BLOCKS + step, BLOCKS)

    def flag(condition):
        return jnp.where(condition, 1, 0)

    cross = {
        1: flag(spot == HALF_RING - 1),
        2: flag(spot >= HALF_RING - 2),
        -1: flag(spot == 0),
        -2: flag(spot <= 1),
    }

    def flip(value, bit):
        return value + bit - 2 * value * bit

    def slot_of(quarter):
        return 2 * flip(quarter // 2, p) + flip(quarter % 2, k)

    def remote(source, target, sends, receives, kind, sort, n, device):
        return pltpu.make_async_remote_copy(
            src_ref=source,
            dst_ref=target,
            send_sem=sends.at[kind, n],
            recv_sem=receives.at[sort, n],
            device_id=device,
            device_id_type=MESH,
        )

    other_core = (c, 2 * p + 1 - k)
    other_chip = (c, 2 * (1 - p) + k)

    def load(n):
        lanes = pl.ds(pl.multiple_of(n * LANES, LANES), LANES)
        return pltpu.make_async_copy(orbitals.at[:, :, lanes], stage.at[n], load_sem.at[n])

    def store(n):
        lanes = pl.ds(pl.multiple_of(n * LANES, LANES), LANES)
        return pltpu.make_async_copy(stage.at[n], out.at[:, :, lanes], store_sem.at[n])

    def each(count, step):
        def run(n, carry):
            step(n)
            return carry

        lax.fori_loop(0, count, run, 0)

    each(CHUNKS, lambda n: load(n).start())

    barrier = pltpu.get_barrier_semaphore()

    def greet(band, grid):
        pl.semaphore_signal(barrier, inc=1, device_id=(band, grid), device_id_type=MESH)

    for away in (1, 2, 3):
        greet(c, lax.rem(g + away, 4))
    for step in (1, 2, -1, -2):
        for core in (0, 1):
            greet(block(step), 2 * p + core)

            @pl.when(cross[step] == 1)
            def _(step=step, core=core):
                greet(block(step), 2 * (1 - p) + core)

    pl.semaphore_wait(barrier, 11 + 2 * (cross[1] + cross[2] + cross[-1] + cross[-2]))

    note_out[0:1, :] = jnp.zeros((1, GRID), F32) + occ[p]
    for j in range(2):
        note_out[1 + j : 2 + j, :] = jnp.zeros((1, GRID), F32) + keep[4 * p + j].astype(F32)
    note = pltpu.make_async_remote_copy(
        src_ref=note_out,
        dst_ref=note_in,
        send_sem=note_sem.at[0],
        recv_sem=note_sem.at[1],
        device_id=(lax.rem(c + BLOCKS - 1 + 3 * k, BLOCKS), g),
        device_id_type=MESH,
    )
    note.start()

    def in_exchange(n):
        mine = own.at[n, 0]
        return (
            remote(mine, own.at[n, 2], send_a, recv_a, 0, 2, n, other_chip),
            remote(mine, own.at[n, 1], send_a, recv_a, 1, 1, n, other_core),
            remote(
                own.at[n, 0, p], lead.at[n, k], send_a, recv_a, 2, 3 + k, n, (block(-1), 2 * p)
            ),
            remote(
                own.at[n, 0, p],
                lead.at[n, 1 - k],
                send_a,
                recv_a,
                3,
                4 - k,
                n,
                (block(2), 2 * p + 1),
            ),
        )

    def in_second(n):
        def source(crossing):
            return own.at[n, 2 - 2 * crossing, flip(p, crossing)]

        near, far = cross[-1], cross[2]
        far_slot = jnp.where(odd == 1, 4, 3 - k)
        far_device = (
            lax.rem(c + 2 - odd, BLOCKS),
            2 * flip(p, far) + jnp.where(odd == 1, k, 1),
        )
        return (
            remote(own.at[n, 2], own.at[n, 3], send_a, recv_a, 4, 0, n, other_core),
            remote(
                source(near),
                lead.at[n, 2 + k],
                send_a,
                recv_a,
                5,
                5 + k,
                n,
                (block(-1), 2 * flip(p, near)),
            ),
            remote(
                source(far), lead.at[n, far_slot], send_a, recv_a, 6, 3 + far_slot, n, far_device
            ),
        )

    def in_relay(n):
        return remote(
            lead.at[n, 4], lead.at[n, 3 - k], send_a, recv_a, 7, 6 - k, n, (block(1), 2 * p + 1)
        )

    def arrived_a(ref, sort, n):
        remote(ref, ref, send_a, recv_a, 0, sort, n, other_core).wait_recv()

    def make_factor(n):
        shape = (GRID, GRID)
        rows = lax.broadcasted_iota(jnp.int32, shape, 0)
        columns = lax.broadcasted_iota(jnp.int32, shape, 1)

        def squared(index):
            freq = jnp.where(index >= GRID // 2, index - GRID, index).astype(F32)
            return freq * freq

        base = squared(rows) + squared(columns)

        def plane(i, carry):
            kx = n * (GRID // CHUNKS) + i
            q = (base + squared(jnp.full(shape, kx, jnp.int32))) * (1.0 / WIDTH)
            safe = jnp.where(q > 0, q, 1.0)
            ratio = jnp.where(q > 0, (1.0 - jnp.exp(-safe)) / safe, 1.0)
            factor[kx] = ratio * (4.0 / GRID**3)
            return carry

        lax.fori_loop(0, GRID // CHUNKS, plane, 0)

    def rows_of(y):
        return pl.ds(pl.multiple_of(y * 8, 8), 8)

    def forward(n):
        for pair in range(PAIRS):
            lanes = slice(pair * 2 * GRID, (pair + 1) * 2 * GRID)
            slots = [slot_of(quarter) for quarter in range(4)]
            first = jnp.concatenate([lead[n, s, :, lanes] for s in slots], 0)
            parts = [
                first * jnp.concatenate([own[n, s, j, :, lanes] for s in slots], 0)
                for j in range(2)
            ]
            mixed = regroup(dot(minus[...], jnp.concatenate(parts, 0)).astype(BF))
            result = dot(mixed, plus[...])
            for half in range(2):
                rows = rows_of(n * 2 * PAIRS + 2 * pair + half)
                for t in range(TILES):
                    at = half * GRID + t * 8
                    real[t, rows, :] = result[at : at + 8, :GRID]
                    imag[t, rows, :] = result[at : at + 8, GRID:]

    def in_step(n, carry):
        @pl.when(n < CHUNKS)
        def _():
            load(n).wait()
            own[n, 0] = stage[n].astype(BF)
            for copy in in_exchange(n):
                copy.start()
            make_factor(n)

        @pl.when((n >= 1) & (n < CHUNKS + 1))
        def _():
            arrived_a(own.at[n - 1, 2], 2, n - 1)
            for copy in in_second(n - 1):
                copy.start()

        @pl.when((n >= 2) & (n < CHUNKS + 2) & (odd == 0))
        def _():
            arrived_a(lead.at[n - 2, 4], 7, n - 2)
            in_relay(n - 2).start()

        @pl.when(n >= 3)
        def _():
            m = n - 3
            arrived_a(own.at[m, 1], 1, m)
            arrived_a(own.at[m, 3], 0, m)
            for s in range(4):
                arrived_a(lead.at[m, s], 3 + s, m)
            forward(m)

        return carry

    lax.fori_loop(0, CHUNKS + 3, in_step, 0)

    def middle(step):
        for t in (2 * step, 2 * step + 1):
            for pair in range(4):
                pick = [pl.ds(2 * pair + half, GRID, stride=8) for half in range(2)]
                packed = jnp.concatenate(
                    [jnp.concatenate([w[t, r, :] for r in pick], 1) for w in (real, imag)], 0
                ).astype(BF)
                scale = jnp.concatenate(
                    [factor[t * 8 + 2 * pair], factor[t * 8 + 2 * pair + 1]], 1
                )
                scale = jnp.concatenate([scale, scale], 0)
                field = (dot(minus[...], packed) * scale).astype(BF)
                result = dot(plus[...], field)
                for half in range(2):
                    at = slice(half * GRID, (half + 1) * GRID)
                    real[t, pick[half], :] = result[:GRID, at]
                    imag[t, pick[half], :] = result[GRID:, at]

    each(TILES // 2, middle)

    def in_sent(n):
        for copy in in_exchange(n) + in_second(n):
            copy.wait_send()

        @pl.when(odd == 0)
        def _():
            in_relay(n).wait_send()

    each(CHUNKS, in_sent)

    note.wait()
    weights = []
    for j in range(2):
        kept = jnp.where(k == 0, note_in[1 + j : 2 + j, :], keep[4 * j + 2 + p].astype(F32))
        for amount in (occ[j], note_in[0:1, :]):
            row = -(amount * kept)
            weights.append(jnp.concatenate([row, row], 1))
    own0, lead0, own1, lead1 = weights

    def inverse(n):
        for pair in range(PAIRS):
            lanes = slice(pair * 2 * GRID, (pair + 1) * 2 * GRID)

            def field(w):
                halves = []
                for half in range(2):
                    rows = rows_of(n * 2 * PAIRS + 2 * pair + half)
                    halves.append(jnp.concatenate([w[t, rows, :] for t in range(TILES)], 0))
                return jnp.concatenate(halves, 1)

            packed = jnp.concatenate([field(real), field(imag)], 0).astype(BF)
            mixed = regroup(dot(plus[...], packed).astype(BF))
            potential = dot(mixed, minus[...])
            v0 = jnp.concatenate([potential[:GRID, :GRID], potential[GRID:, :GRID]], 1)
            v1 = jnp.concatenate([potential[:GRID, GRID:], potential[GRID:, GRID:]], 1)
            for quarter in range(4):
                s = slot_of(quarter)
                rows = slice(quarter * SLAB, (quarter + 1) * SLAB)
                x0, x1 = v0[rows], v1[rows]
                a = lead[n, s, :, lanes].astype(F32)
                b0 = own[n, s, 0, :, lanes].astype(F32)
                b1 = own[n, s, 1, :, lanes].astype(F32)
                lead[n, s, :, lanes] = ((own0 * x0) * b0 + (own1 * x1) * b1).astype(BF)
                own[n, s, 0, :, lanes] = ((lead0 * x0) * a).astype(BF)
                own[n, s, 1, :, lanes] = ((lead1 * x1) * a).astype(BF)

    home = lax.rem(c + BLOCKS + 1 - 3 * k, BLOCKS)
    home_cross = jnp.where(k == 0, cross[1], cross[-2])
    hop = k * (1 - odd)

    def out_first(n):
        far = 2 * flip(p, home_cross)
        target = lax.rem(home + hop, BLOCKS)
        return (
            remote(own.at[n, 1], core_in.at[n, 0], send_b, recv_b, 0, 0, n, other_core),
            remote(own.at[n, 3], core_in.at[n, 1], send_b, recv_b, 1, 1, n, other_core),
            remote(lead.at[n, 0], near_in.at[n, k], send_b, recv_b, 2, 2 + k, n, (home, g)),
            remote(
                lead.at[n, 1],
                near_in.at[n, k],
                send_b,
                recv_b,
                3,
                2 + k,
                n,
                (home, 2 * p + 1 - k),
            ),
            remote(
                lead.at[n, 2],
                far_in.at[n, k + hop],
                send_b,
                recv_b,
                4,
                4 + k + hop,
                n,
                (target, far + k),
            ),
            remote(
                lead.at[n, 3],
                far_in.at[n, k + hop],
                send_b,
                recv_b,
                5,
                4 + k + hop,
                n,
                (target, far + 1 - k),
            ),
        )

    def out_relay(n):
        return remote(
            far_in.at[n, 2], far_in.at[n, 1], send_b, recv_b, 6, 5, n, (block(-1), g)
        )

    def out_chip(n):
        return remote(own.at[n, 2], chip_in.at[n], send_b, recv_b, 7, 7, n, other_chip)

    def arrived_b(ref, sort, n):
        remote(ref, ref, send_b, recv_b, 0, sort, n, other_core).wait_recv()

    straight = [cross[-1].astype(F32), cross[2].astype(F32)]

    def out_step(n, carry):
        @pl.when(n < CHUNKS)
        def _():
            inverse(n)
            for copy in out_first(n):
                copy.start()

        @pl.when((n >= 1) & (n < CHUNKS + 1) & (odd == 1))
        def _():
            arrived_b(far_in.at[n - 1, 2], 6, n - 1)
            out_relay(n - 1).start()

        @pl.when((n >= 2) & (n < CHUNKS + 2))
        def _():
            m = n - 2
            arrived_b(core_in.at[m, 1], 1, m)
            arrived_b(far_in.at[m, 0], 4, m)
            arrived_b(far_in.at[m, 1], 5, m)
            sums = own[m, 2].astype(F32) + core_in[m, 1].astype(F32)
            own[m, 2] = sums.astype(BF)
            extra = (1.0 - straight[0]) * far_in[m, 0].astype(F32) + (
                1.0 - straight[1]
            ) * far_in[m, 1].astype(F32)
            mine = jnp.where(p == 0, sums[0], sums[1])
            own[m, 2, p] = (mine + extra).astype(BF)
            out_chip(m).start()

        @pl.when(n >= 4)
        def _():
            m = n - 4
            arrived_b(core_in.at[m, 0], 0, m)
            arrived_b(near_in.at[m, 0], 2, m)
            arrived_b(near_in.at[m, 1], 3, m)
            arrived_b(chip_in.at[m], 7, m)

            def total(band):
                return (
                    own[m, 0, band].astype(F32)
                    + core_in[m, 0, band].astype(F32)
                    + chip_in[m, band].astype(F32)
                )

            extra = straight[0] * far_in[m, 0].astype(F32) + straight[1] * far_in[m, 1].astype(
                F32
            )
            stage[m, p] = (
                total(p) + near_in[m, 0].astype(F32) + near_in[m, 1].astype(F32)
            )
            stage[m, 1 - p] = total(1 - p) + extra
            store(m).start()

        return carry

    lax.fori_loop(0, CHUNKS + 4, out_step, 0)

    def out_sent(n):
        for copy in out_first(n) + (out_chip(n),):
            copy.wait_send()

        @pl.when(odd == 1)
        def _():
            out_relay(n).wait_send()

        store(n).wait()

    each(CHUNKS, out_sent)


def body(orbitals, occupation, pair_keep):
    plus, minus = tables()
    vmem = pl.BlockSpec(memory_space=pltpu.VMEM)
    smem = pl.BlockSpec(memory_space=pltpu.SMEM)
    anywhere = pl.BlockSpec(memory_space=pl.ANY)
    dma = pltpu.SemaphoreType.DMA
    return pl.pallas_call(
        kernel,
        out_shape=jax.ShapeDtypeStruct(orbitals.shape, F32),
        in_specs=[smem, smem, anywhere, vmem, vmem],
        out_specs=anywhere,
        scratch_shapes=[
            pltpu.VMEM((CHUNKS, 2, SLAB, LANES), F32),
            pltpu.VMEM((CHUNKS, 5, SLAB, LANES), BF),
            pltpu.VMEM((CHUNKS, 4, 2, SLAB, LANES), BF),
            pltpu.VMEM((TILES, 8 * GRID, GRID), F32),
            pltpu.VMEM((TILES, 8 * GRID, GRID), F32),
            pltpu.VMEM((GRID, GRID, GRID), F32),
            pltpu.VMEM((CHUNKS, 2, SLAB, LANES), BF),
            pltpu.VMEM((CHUNKS, 3, SLAB, LANES), BF),
            pltpu.VMEM((CHUNKS, 2, 2, SLAB, LANES), BF),
            pltpu.VMEM((CHUNKS, 2, SLAB, LANES), BF),
            pltpu.VMEM((8, GRID), F32),
            pltpu.VMEM((8, GRID), F32),
            dma((CHUNKS,)),
            dma((CHUNKS,)),
            dma((8, CHUNKS)),
            dma((8, CHUNKS)),
            dma((8, CHUNKS)),
            dma((8, CHUNKS)),
            dma((2,)),
        ],
        compiler_params=pltpu.CompilerParams(
            collective_id=0, has_side_effects=True, vmem_limit_bytes=60 * 1024 * 1024
        ),
        name="exchange",
    )(occupation, pair_keep.reshape(-1), orbitals, jnp.asarray(plus), jnp.asarray(minus))


def solution(mesh):
    in_specs = (P("band", "grid", None), P("band"), P("band", None, None))
    return jax.shard_map(
        body, mesh=mesh, in_specs=in_specs, out_specs=P("band", "grid", None), check_vma=False
    )
```

```python
import functools
import math

import jax
import jax.numpy as jnp
import numpy as np
from jax import lax
from jax.experimental import pallas as pl
from jax.experimental.pallas import tpu as pltpu
from jax.sharding import PartitionSpec as P

GRID = 128
SLAB = 32
BLOCKS = 32
HALF_RING = 16
WIDTH = 64.0
CHUNKS = 16
LANES = GRID * GRID // CHUNKS
PAIRS = LANES // (2 * GRID)
TILES = GRID // 8
BF = jnp.bfloat16
F32 = jnp.float32
MESH = pl.DeviceIdType.MESH


def tables():
    index = np.arange(GRID)
    angle = (index[:, None] * index[None, :] % GRID) * (2.0 * math.pi / GRID)
    cosine, sine = np.cos(angle), np.sin(angle)
    forward = np.block([[cosine, -sine], [sine, cosine]])
    return tuple(np.asarray(t, np.float32).astype(BF) for t in (forward, forward.T))


def dot(left, right):
    return jnp.dot(left, right, preferred_element_type=F32)


def regroup(value):
    n = GRID
    top = jnp.concatenate([value[:n, :n], value[n:, :n]], 1)
    low = jnp.concatenate([value[:n, n:], value[n:, n:]], 1)
    return jnp.concatenate([top, low], 0)


def kernel(
    occ, keep, orbitals, plus, minus, out,
    stage, lead, own, real, imag, factor, sums_in, core_in, chip_in, note_out, note_in,
    load_sem, store_sem, send_a, recv_a, send_b, recv_b, note_sem,
):
    c, g = lax.axis_index("band"), lax.axis_index("grid")
    p, k = lax.div(g, 2), lax.rem(g, 2)
    spot = lax.rem(c, HALF_RING)
    odd = lax.rem(c, 2)

    def block(step):
        return lax.rem(c + BLOCKS + step, BLOCKS)

    def flag(condition):
        return jnp.where(condition, 1, 0)

    cross = {
        1: flag(spot == HALF_RING - 1),
        2: flag(spot >= HALF_RING - 2),
        -1: flag(spot == 0),
        -2: flag(spot <= 1),
    }

    def flip(value, bit):
        return value + bit - 2 * value * bit

    def slot_of(quarter):
        return 2 * flip(quarter // 2, p) + flip(quarter % 2, k)

    def remote(source, target, sends, receives, kind, sort, n, device):
        return pltpu.make_async_remote_copy(
            src_ref=source,
            dst_ref=target,
            send_sem=sends.at[kind],
            recv_sem=receives.at[sort, n],
            device_id=device,
            device_id_type=MESH,
        )

    other_core = (c, 2 * p + 1 - k)
    other_chip = (c, 2 * (1 - p) + k)

    def load(n):
        lanes = pl.ds(pl.multiple_of(n * LANES, LANES), LANES)
        return pltpu.make_async_copy(orbitals.at[:, :, lanes], stage.at[n], load_sem.at[0])

    def store(n):
        lanes = pl.ds(pl.multiple_of(n * LANES, LANES), LANES)
        return pltpu.make_async_copy(stage.at[n], out.at[:, :, lanes], store_sem.at[0])

    def each(count, step):
        def run(n, carry):
            step(n)
            return carry

        lax.fori_loop(0, count, run, 0)

    each(CHUNKS, lambda n: load(n).start())

    barrier = pltpu.get_barrier_semaphore()

    def greet(band, grid):
        pl.semaphore_signal(barrier, inc=1, device_id=(band, grid), device_id_type=MESH)

    for away in (1, 2, 3):
        greet(c, lax.rem(g + away, 4))
    for step in (1, 2, -1, -2):
        for core in (0, 1):
            greet(block(step), 2 * p + core)

            @pl.when(cross[step] == 1)
            def _(step=step, core=core):
                greet(block(step), 2 * (1 - p) + core)

    pl.semaphore_wait(barrier, 11 + 2 * (cross[1] + cross[2] + cross[-1] + cross[-2]))

    note_out[0:1, :] = jnp.zeros((1, GRID), F32) + occ[p]
    for j in range(2):
        note_out[1 + j : 2 + j, :] = jnp.zeros((1, GRID), F32) + keep[p, 0, j].astype(F32)
    note = pltpu.make_async_remote_copy(
        src_ref=note_out,
        dst_ref=note_in,
        send_sem=note_sem.at[0],
        recv_sem=note_sem.at[1],
        device_id=(lax.rem(c + BLOCKS - 1 + 3 * k, BLOCKS), g),
        device_id_type=MESH,
    )
    note.start()

    def in_first(n):
        near, far = cross[-1], cross[2]
        mine = own.at[n, 0]
        return (
            remote(mine, own.at[n, 2], send_a, recv_a, 0, 0, n, other_chip),
            remote(mine, own.at[n, 1], send_a, recv_a, 1, 1, n, other_core),
            remote(
                own.at[n, 0, flip(p, near)],
                lead.at[n, k + 2 * near],
                send_a,
                recv_a,
                2,
                1,
                n,
                (block(-1), 2 * flip(p, near)),
            ),
            remote(
                own.at[n, 0, flip(p, far)],
                lead.at[n, 1 - k + 2 * far],
                send_a,
                recv_a,
                3,
                1,
                n,
                (block(2), 2 * flip(p, far) + 1),
            ),
        )

    def in_second(n):
        near, far = cross[-1], cross[2]
        return (
            remote(own.at[n, 2], own.at[n, 3], send_a, recv_a, 4, 1, n, other_core),
            remote(
                own.at[n, 2, flip(p, near)],
                lead.at[n, k + 2 - 2 * near],
                send_a,
                recv_a,
                5,
                1,
                n,
                (block(-1), 2 * flip(p, near)),
            ),
            remote(
                own.at[n, 2, flip(p, far)],
                lead.at[n, jnp.where(odd == 1, 4, 3 - k - 2 * far)],
                send_a,
                recv_a,
                6,
                1 + odd,
                n,
                (lax.rem(c + 2 - odd, BLOCKS), 2 * flip(p, far) + jnp.where(odd == 1, k, 1)),
            ),
        )

    def in_relay(n):
        return remote(
            lead.at[n, 4],
            lead.at[n, 3 - k - 2 * cross[-1]],
            send_a,
            recv_a,
            7,
            1,
            n,
            (block(1), 2 * p + 1),
        )

    def sent(ref, sends, kind):
        pltpu.make_async_remote_copy(
            src_ref=ref,
            dst_ref=ref,
            send_sem=sends.at[kind],
            recv_sem=note_sem.at[1],
            device_id=other_core,
            device_id_type=MESH,
        ).wait_send()

    def arrived_a(ref, sort, n):
        remote(ref, ref, send_a, recv_a, 0, sort, n, other_core).wait_recv()

    def make_factor(n):
        shape = (GRID, GRID)
        rows = lax.broadcasted_iota(jnp.int32, shape, 0)
        columns = lax.broadcasted_iota(jnp.int32, shape, 1)

        def squared(index):
            freq = jnp.where(index >= GRID // 2, index - GRID, index).astype(F32)
            return freq * freq

        base = squared(rows) + squared(columns)

        def plane(i, carry):
            kx = n * (GRID // CHUNKS) + i
            q = (base + squared(jnp.full(shape, kx, jnp.int32))) * (1.0 / WIDTH)
            safe = jnp.where(q > 0, q, 1.0)
            ratio = jnp.where(q > 0, (1.0 - jnp.exp(-safe)) / safe, 1.0)
            factor[kx] = ratio * (4.0 / GRID**3)
            return carry

        lax.fori_loop(0, GRID // CHUNKS, plane, 0)

    def rows_of(y):
        return pl.ds(pl.multiple_of(y * 8, 8), 8)

    def forward(n):
        for pair in range(PAIRS):
            lanes = slice(pair * 2 * GRID, (pair + 1) * 2 * GRID)
            slots = [slot_of(quarter) for quarter in range(4)]
            first = jnp.concatenate([lead[n, s, :, lanes] for s in slots], 0)
            parts = [
                first * jnp.concatenate([own[n, s, j, :, lanes] for s in slots], 0)
                for j in range(2)
            ]
            mixed = regroup(dot(minus[...], jnp.concatenate(parts, 0)).astype(BF))
            result = dot(mixed, plus[...])
            for half in range(2):
                rows = rows_of(n * 2 * PAIRS + 2 * pair + half)
                for t in range(TILES):
                    at = half * GRID + t * 8
                    real[t, rows, :] = result[at : at + 8, :GRID]
                    imag[t, rows, :] = result[at : at + 8, GRID:]

    pltpu.make_async_copy(stage, stage, load_sem.at[0]).wait()

    def in_step(n, carry):
        @pl.when(n < CHUNKS)
        def _():
            own[n, 0] = stage[n].astype(BF)
            for copy in in_first(n):
                copy.start()
            make_factor(n)

        @pl.when((n >= 1) & (n < CHUNKS + 1))
        def _():
            arrived_a(own.at[n - 1, 2], 0, n - 1)
            for copy in in_second(n - 1):
                copy.start()

        @pl.when((n >= 2) & (n < CHUNKS + 2) & (odd == 0))
        def _():
            arrived_a(lead.at[n - 2, 4], 2, n - 2)
            in_relay(n - 2).start()

        @pl.when(n >= 3)
        def _():
            arrived_a(own.at[n - 3], 1, n - 3)
            forward(n - 3)

        return carry

    lax.fori_loop(0, CHUNKS + 3, in_step, 0)

    def middle(step):
        for t in (4 * step + i for i in range(4)):
            for pair in range(4):
                pick = [pl.ds(2 * pair + half, GRID, stride=8) for half in range(2)]
                packed = jnp.concatenate(
                    [jnp.concatenate([w[t, r, :] for r in pick], 1) for w in (real, imag)], 0
                ).astype(BF)
                scale = jnp.concatenate(
                    [factor[t * 8 + 2 * pair], factor[t * 8 + 2 * pair + 1]], 1
                )
                scale = jnp.concatenate([scale, scale], 0)
                field = (dot(minus[...], packed) * scale).astype(BF)
                result = dot(plus[...], field)
                for half in range(2):
                    at = slice(half * GRID, (half + 1) * GRID)
                    real[t, pick[half], :] = result[:GRID, at]
                    imag[t, pick[half], :] = result[GRID:, at]

    each(TILES // 4, middle)

    for kind, ref in enumerate(
        (own.at[:, 0],) * 2 + (own.at[:, 0, 0],) * 2 + (own.at[:, 2],) + (own.at[:, 2, 0],) * 2
    ):
        sent(ref, send_a, kind)

    @pl.when(odd == 0)
    def _():
        sent(lead.at[:, 4], send_a, 7)

    note.wait()
    weights = []
    for j in range(2):
        kept = jnp.where(k == 0, note_in[1 + j : 2 + j, :], keep[j, 1, p].astype(F32))
        for amount in (occ[j], note_in[0:1, :]):
            row = -(amount * kept)
            weights.append(jnp.concatenate([row, row], 1))
    own0, lead0, own1, lead1 = weights

    def inverse(n):
        for pair in range(PAIRS):
            lanes = slice(pair * 2 * GRID, (pair + 1) * 2 * GRID)

            def field(w):
                halves = []
                for half in range(2):
                    rows = rows_of(n * 2 * PAIRS + 2 * pair + half)
                    halves.append(jnp.concatenate([w[t, rows, :] for t in range(TILES)], 0))
                return jnp.concatenate(halves, 1)

            packed = jnp.concatenate([field(real), field(imag)], 0).astype(BF)
            mixed = regroup(dot(plus[...], packed).astype(BF))
            potential = dot(mixed, minus[...])
            v0 = jnp.concatenate([potential[:GRID, :GRID], potential[GRID:, :GRID]], 1)
            v1 = jnp.concatenate([potential[:GRID, GRID:], potential[GRID:, GRID:]], 1)
            for quarter in range(4):
                s = slot_of(quarter)
                rows = slice(quarter * SLAB, (quarter + 1) * SLAB)
                x0, x1 = v0[rows], v1[rows]
                a = lead[n, s, :, lanes].astype(F32)
                b0 = own[n, s, 0, :, lanes].astype(F32)
                b1 = own[n, s, 1, :, lanes].astype(F32)
                lead[n, s, :, lanes] = ((own0 * x0) * b0 + (own1 * x1) * b1).astype(BF)
                own[n, s, 0, :, lanes] = ((lead0 * x0) * a).astype(BF)
                own[n, s, 1, :, lanes] = ((lead1 * x1) * a).astype(BF)

    home = lax.rem(c + BLOCKS + 1 - 3 * k, BLOCKS)
    home_cross = jnp.where(k == 0, cross[1], cross[-2])
    hop = k * (1 - odd)

    def out_first(n):
        chip = 2 * flip(p, home_cross)

        def lead_out(slot, core):
            away = slot // 2
            hands_on = flip(away, home_cross)
            relayed = away * hop
            kind = k + 2 * hands_on + relayed * (4 - k - 2 * hands_on)
            device = (lax.rem(home + relayed, BLOCKS), chip + core)
            sort = (1 - hands_on) * (1 - relayed) + 2 * relayed
            return remote(
                lead.at[n, slot], sums_in.at[n, kind], send_b, recv_b, 2 + slot, sort, n, device
            )

        return (
            remote(own.at[n, 1], core_in.at[n, 0], send_b, recv_b, 0, 1, n, other_core),
            remote(own.at[n, 3], core_in.at[n, 1], send_b, recv_b, 1, 0, n, other_core),
            lead_out(0, k),
            lead_out(1, 1 - k),
            lead_out(2, k),
            lead_out(3, 1 - k),
        )

    def out_relay(n):
        return remote(
            sums_in.at[n, 4],
            sums_in.at[n, 3 - 2 * cross[1]],
            send_b,
            recv_b,
            6,
            cross[1],
            n,
            (block(-1), g),
        )

    def out_chip(n):
        return remote(own.at[n, 2], chip_in.at[n], send_b, recv_b, 7, 3, n, other_chip)

    def arrived_b(ref, sort, n):
        remote(ref, ref, send_b, recv_b, 0, sort, n, other_core).wait_recv()

    bands = [flip(p, cross[-1]), flip(p, cross[2])]
    masks = [[flag(b == band).astype(F32) for b in bands] for band in range(2)]

    def lead_sums(m, first, band):
        return masks[band][0] * sums_in[m, first].astype(F32) + masks[band][1] * sums_in[
            m, first + 1
        ].astype(F32)

    def out_step(n, carry):
        @pl.when(n < CHUNKS)
        def _():
            inverse(n)
            for copy in out_first(n):
                copy.start()

        @pl.when((n >= 1) & (n < CHUNKS + 1) & (odd == 1))
        def _():
            arrived_b(sums_in.at[n - 1, 4], 2, n - 1)
            out_relay(n - 1).start()

        @pl.when((n >= 2) & (n < CHUNKS + 2))
        def _():
            m = n - 2
            arrived_b(core_in.at[m], 0, m)
            for band in range(2):
                total = own[m, 2, band].astype(F32) + core_in[m, 1, band].astype(F32)
                own[m, 2, band] = (total + lead_sums(m, 2, band)).astype(BF)
            out_chip(m).start()

        @pl.when(n >= 4)
        def _():
            m = n - 4
            arrived_b(core_in.at[m], 1, m)
            arrived_b(chip_in.at[m], 3, m)
            for band in range(2):
                total = own[m, 0, band].astype(F32) + core_in[m, 0, band].astype(F32)
                stage[m, band] = (
                    total + chip_in[m, band].astype(F32) + lead_sums(m, 0, band)
                )
            store(m).start()

        return carry

    lax.fori_loop(0, CHUNKS + 4, out_step, 0)

    for kind, ref in enumerate((own.at[:, 0],) * 2 + (lead.at[:, 0],) * 4):
        sent(ref, send_b, kind)

    @pl.when(odd == 1)
    def _():
        sent(sums_in.at[:, 4], send_b, 6)

    sent(own.at[:, 2], send_b, 7)
    pltpu.make_async_copy(stage, stage, store_sem.at[0]).wait()


def body(orbitals, occupation, pair_keep):
    plus, minus = tables()
    vmem = pl.BlockSpec(memory_space=pltpu.VMEM)
    smem = pl.BlockSpec(memory_space=pltpu.SMEM)
    anywhere = pl.BlockSpec(memory_space=pl.ANY)
    dma = pltpu.SemaphoreType.DMA
    return pl.pallas_call(
        kernel,
        out_shape=jax.ShapeDtypeStruct(orbitals.shape, F32),
        in_specs=[smem, smem, anywhere, vmem, vmem],
        out_specs=anywhere,
        scratch_shapes=[
            pltpu.VMEM((CHUNKS, 2, SLAB, LANES), F32),
            pltpu.VMEM((CHUNKS, 5, SLAB, LANES), BF),
            pltpu.VMEM((CHUNKS, 4, 2, SLAB, LANES), BF),
            pltpu.VMEM((TILES, 8 * GRID, GRID), F32),
            pltpu.VMEM((TILES, 8 * GRID, GRID), F32),
            pltpu.VMEM((GRID, GRID, GRID), F32),
            pltpu.VMEM((CHUNKS, 5, SLAB, LANES), BF),
            pltpu.VMEM((CHUNKS, 2, 2, SLAB, LANES), BF),
            pltpu.VMEM((CHUNKS, 2, SLAB, LANES), BF),
            pltpu.VMEM((8, GRID), F32),
            pltpu.VMEM((8, GRID), F32),
            dma((1,)),
            dma((1,)),
            dma((8,)),
            dma((3, CHUNKS)),
            dma((8,)),
            dma((4, CHUNKS)),
            dma((2,)),
        ],
        compiler_params=pltpu.CompilerParams(
            collective_id=0, has_side_effects=True, vmem_limit_bytes=60 * 1024 * 1024
        ),
        name="exchange",
    )(occupation, pair_keep, orbitals, jnp.asarray(plus), jnp.asarray(minus))


def solution(mesh):
    in_specs = (P("band", "grid", None), P("band"), P("band", None, None))
    return jax.shard_map(
        body, mesh=mesh, in_specs=in_specs, out_specs=P("band", "grid", None), check_vma=False
    )
```

```python
import functools
import math

import jax
import jax.numpy as jnp
import numpy as np
from jax import lax
from jax.experimental import pallas as pl
from jax.experimental.pallas import tpu as pltpu
from jax.sharding import PartitionSpec as P

GRID = 128
SLAB = 32
BLOCKS = 32
HALF_RING = 16
WIDTH = 64.0
CHUNKS = 16
LANES = GRID * GRID // CHUNKS
PAIRS = LANES // (2 * GRID)
TILES = GRID // 8
IN_LAGS = (2, 4, 8)
OUT_LAGS = (2, 2, 3, 5)
THIRDS = sum(n % 3 == 2 for n in range(CHUNKS))
BF = jnp.bfloat16
F32 = jnp.float32
MESH = pl.DeviceIdType.MESH


def tables():
    index = np.arange(GRID)
    angle = (index[:, None] * index[None, :] % GRID) * (2.0 * math.pi / GRID)
    cosine, sine = np.cos(angle), np.sin(angle)
    forward = np.block([[cosine, -sine], [sine, cosine]])
    return tuple(np.asarray(t, np.float32).astype(BF) for t in (forward, forward.T))


def dot(left, right):
    return jnp.dot(left, right, preferred_element_type=F32)


def regroup(value):
    n = GRID
    top = jnp.concatenate([value[:n, :n], value[n:, :n]], 1)
    low = jnp.concatenate([value[:n, n:], value[n:, n:]], 1)
    return jnp.concatenate([top, low], 0)


def kernel(
    occ, keep, orbitals, plus, minus, out,
    stage, lead, own, real, imag, factor, sums_in, core_in, chip_in, note_out, note_in,
    load_sem, store_sem, send_a, recv_a, send_b, recv_b, note_sem,
):
    c, g = lax.axis_index("band"), lax.axis_index("grid")
    p, k = lax.div(g, 2), lax.rem(g, 2)
    spot = lax.rem(c, HALF_RING)
    z = lax.rem(c, 4)

    def block(step):
        return lax.rem(c + BLOCKS + step, BLOCKS)

    def flag(condition):
        return jnp.where(condition, 1, 0)

    cross = {
        step: flag(spot >= HALF_RING - step) if step > 0 else flag(spot < -step)
        for step in (1, 2, 3, -1, -2, -3)
    }

    def flip(value, bit):
        return value + bit - 2 * value * bit

    def slot_of(quarter):
        return 2 * flip(quarter // 2, p) + flip(quarter % 2, k)

    def remote(source, target, sends, receives, kind, sort, n, device):
        return pltpu.make_async_remote_copy(
            src_ref=source,
            dst_ref=target,
            send_sem=sends.at[kind],
            recv_sem=receives.at[sort, n],
            device_id=device,
            device_id_type=MESH,
        )

    other_core = (c, 2 * p + 1 - k)
    other_chip = (c, 2 * (1 - p) + k)

    def load(n):
        lanes = pl.ds(pl.multiple_of(n * LANES, LANES), LANES)
        return pltpu.make_async_copy(orbitals.at[:, :, lanes], stage.at[n], load_sem.at[0])

    def store(n):
        lanes = pl.ds(pl.multiple_of(n * LANES, LANES), LANES)
        return pltpu.make_async_copy(stage.at[n], out.at[:, :, lanes], store_sem.at[0])

    def each(count, step):
        def run(n, carry):
            step(n)
            return carry

        lax.fori_loop(0, count, run, 0)

    each(CHUNKS, lambda n: load(n).start())

    def clear(n):
        @pl.when((k == 0) | (lax.rem(n, 3) == 2))
        def _():
            sums_in[n, 2] = jnp.zeros((SLAB, LANES), BF)

    each(CHUNKS, clear)

    barrier = pltpu.get_barrier_semaphore()

    def greet(band, grid):
        pl.semaphore_signal(barrier, inc=1, device_id=(band, grid), device_id_type=MESH)

    for away in (1, 2, 3):
        greet(c, lax.rem(g + away, 4))
    for step in cross:
        for core in (0, 1):
            greet(block(step), 2 * p + core)

            @pl.when(cross[step] == 1)
            def _(step=step, core=core):
                greet(block(step), 2 * (1 - p) + core)

    pl.semaphore_wait(barrier, 15 + 2 * sum(cross.values()))

    note_out[...] = jnp.zeros((8, GRID), F32) + occ[p]
    note = pltpu.make_async_remote_copy(
        src_ref=note_out,
        dst_ref=note_in,
        send_sem=note_sem.at[0],
        recv_sem=note_sem.at[1],
        device_id=(lax.rem(c + 1 + k, BLOCKS), g),
        device_id_type=MESH,
    )
    note.start()

    def third(n):
        return lax.rem(n, 3) == 2

    def in_bands(n):
        mine = own.at[n, 0]
        return (
            remote(mine, own.at[n, 2], send_a, recv_a, 0, 0, n, other_chip),
            remote(mine, own.at[n, 1], send_a, recv_a, 1, 1, n, other_core),
        )

    def in_core(n):
        return remote(own.at[n, 2], own.at[n, 3], send_a, recv_a, 4, 1, n, other_core)

    def in_one(n, far):
        chip = flip(p, cross[1])
        return remote(
            own.at[n, 2 * flip(far, cross[1]), chip],
            lead.at[n, k + 2 * far],
            send_a,
            recv_a,
            2 + far,
            2 - far,
            n,
            (block(1), 2 * chip),
        )

    def in_two(n, far):
        chip = flip(p, cross[2])
        direct = z == 1
        step = jnp.where(direct, 2, jnp.where(z == 0, 3, -1))
        device = jnp.where(direct, 2 * chip + 1, g)
        return remote(
            own.at[n, 2 * flip(far, cross[2]), chip],
            lead.at[n, jnp.where(direct, 1 - k + 2 * far, 4 + far)],
            send_a,
            recv_a,
            5 + far,
            jnp.where(direct, 2 - far, 3 + far),
            n,
            (block(step), device),
        )

    in_between = z != 0

    def in_pass(n, far):
        chip = flip(p, flag((spot == HALF_RING - 3) | (spot == HALF_RING - 2)))
        return remote(
            lead.at[n, 4 + far],
            lead.at[n, 1 - k + 2 * far],
            send_a,
            recv_a,
            7 + far,
            2 - far,
            n,
            (block(jnp.where(z == 3, -1, 3)), 2 * chip + 1),
        )

    def in_share(n, slot):
        return remote(
            lead.at[n, slot],
            lead.at[n, 1 - slot],
            send_a,
            recv_a,
            9 + slot,
            2,
            n,
            (block(1), 2 * p + 1),
        )

    def in_leads(n, second):
        in_one(n, flip(second, cross[1])).start()
        far = flip(second, cross[2])

        @pl.when((far == 1) | ((k == 1) & jnp.logical_not(third(n))))
        def _():
            in_two(n, far).start()

    def sent(ref, sends, kind):
        pltpu.make_async_remote_copy(
            src_ref=ref,
            dst_ref=ref,
            send_sem=sends.at[kind],
            recv_sem=note_sem.at[1],
            device_id=other_core,
            device_id_type=MESH,
        ).wait_send()

    def arrived_a(ref, sort, n):
        remote(ref, ref, send_a, recv_a, 0, sort, n, other_core).wait_recv()

    def make_factor(n):
        shape = (GRID, GRID)
        rows = lax.broadcasted_iota(jnp.int32, shape, 0)
        columns = lax.broadcasted_iota(jnp.int32, shape, 1)

        def squared(index):
            freq = jnp.where(index >= GRID // 2, index - GRID, index).astype(F32)
            return freq * freq

        base = squared(rows) + squared(columns)

        def plane(i, carry):
            kx = n * (GRID // CHUNKS) + i
            q = (base + squared(jnp.full(shape, kx, jnp.int32))) * (1.0 / WIDTH)
            safe = jnp.where(q > 0, q, 1.0)
            ratio = jnp.where(q > 0, (1.0 - jnp.exp(-safe)) / safe, 1.0)
            factor[kx] = ratio * (4.0 / GRID**3)
            return carry

        lax.fori_loop(0, GRID // CHUNKS, plane, 0)

    def rows_of(y):
        return pl.ds(pl.multiple_of(y * 8, 8), 8)

    def forward(n):
        for pair in range(PAIRS):
            lanes = slice(pair * 2 * GRID, (pair + 1) * 2 * GRID)
            slots = [slot_of(quarter) for quarter in range(4)]
            first = jnp.concatenate([lead[n, s, :, lanes] for s in slots], 0)
            parts = [
                first * jnp.concatenate([own[n, s, j, :, lanes] for s in slots], 0)
                for j in range(2)
            ]
            mixed = regroup(dot(minus[...], jnp.concatenate(parts, 0)).astype(BF))
            result = dot(mixed, plus[...])
            for half in range(2):
                rows = rows_of(n * 2 * PAIRS + 2 * pair + half)
                for t in range(TILES):
                    at = half * GRID + t * 8
                    real[t, rows, :] = result[at : at + 8, :GRID]
                    imag[t, rows, :] = result[at : at + 8, GRID:]

    pltpu.make_async_copy(stage, stage, load_sem.at[0]).wait()

    def in_step(n, carry):
        @pl.when(n < CHUNKS)
        def _():
            own[n, 0] = stage[n].astype(BF)
            for copy in in_bands(n):
                copy.start()
            in_leads(n, 0)
            make_factor(n)

        @pl.when((n >= IN_LAGS[0]) & (n < CHUNKS + IN_LAGS[0]))
        def _():
            m = n - IN_LAGS[0]
            arrived_a(own.at[m, 2], 0, m)
            in_leads(m, 1)
            in_core(m).start()

        @pl.when((n >= IN_LAGS[1]) & (n < CHUNKS + IN_LAGS[1]))
        def _():
            m = n - IN_LAGS[1]

            @pl.when(in_between)
            def _():
                arrived_a(lead.at[m, 5], 4, m)
                in_pass(m, 1).start()

                @pl.when((k == 1) & jnp.logical_not(third(m)))
                def _():
                    arrived_a(lead.at[m, 4], 3, m)
                    in_pass(m, 0).start()

            @pl.when(k == 0)
            def _():
                arrived_a(lead.at[m, 0:2], 2, m)
                in_share(m, 0).start()

                @pl.when(third(m))
                def _():
                    in_share(m, 1).start()

        @pl.when(n >= IN_LAGS[2])
        def _():
            m = n - IN_LAGS[2]

            @pl.when(k == 1)
            def _():
                arrived_a(lead.at[m, 0:2], 2, m)

            arrived_a(own.at[m, 0:3], 1, m)
            forward(m)

        return carry

    lax.fori_loop(0, CHUNKS + IN_LAGS[2], in_step, 0)

    def middle(step):
        for t in (4 * step + i for i in range(4)):
            for pair in range(4):
                pick = [pl.ds(2 * pair + half, GRID, stride=8) for half in range(2)]
                packed = jnp.concatenate(
                    [jnp.concatenate([w[t, r, :] for r in pick], 1) for w in (real, imag)], 0
                ).astype(BF)
                scale = jnp.concatenate(
                    [factor[t * 8 + 2 * pair], factor[t * 8 + 2 * pair + 1]], 1
                )
                scale = jnp.concatenate([scale, scale], 0)
                field = (dot(minus[...], packed) * scale).astype(BF)
                result = dot(plus[...], field)
                for half in range(2):
                    at = slice(half * GRID, (half + 1) * GRID)
                    real[t, pick[half], :] = result[:GRID, at]
                    imag[t, pick[half], :] = result[GRID:, at]

    each(TILES // 4, middle)

    one, some, rest = lead.at[:, 0], lead.at[:THIRDS, 0], lead.at[THIRDS:, 0]
    for kind, ref in enumerate((own.at[:, 0], own.at[:, 0], one, one, own.at[:, 2])):
        sent(ref, send_a, kind)
    sent(one, send_a, 6)

    @pl.when(k == 1)
    def _():
        sent(rest, send_a, 5)

    @pl.when(k == 0)
    def _():
        sent(one, send_a, 9)
        sent(some, send_a, 10)

    @pl.when(in_between)
    def _():
        sent(one, send_a, 8)

        @pl.when(k == 1)
        def _():
            sent(rest, send_a, 7)

    note.wait()
    kept = [keep[j, k, p].astype(F32) for j in range(2)]
    own0, own1 = (-(occ[j] * kept[j]) for j in range(2))
    amount = jnp.concatenate([note_in[0:1, :]] * 2, 1)
    lead0, lead1 = (-(amount * kept[j]) for j in range(2))

    def inverse(n):
        for pair in range(PAIRS):
            lanes = slice(pair * 2 * GRID, (pair + 1) * 2 * GRID)

            def field(w):
                halves = []
                for half in range(2):
                    rows = rows_of(n * 2 * PAIRS + 2 * pair + half)
                    halves.append(jnp.concatenate([w[t, rows, :] for t in range(TILES)], 0))
                return jnp.concatenate(halves, 1)

            packed = jnp.concatenate([field(real), field(imag)], 0).astype(BF)
            mixed = regroup(dot(plus[...], packed).astype(BF))
            potential = dot(mixed, minus[...])
            v0 = jnp.concatenate([potential[:GRID, :GRID], potential[GRID:, :GRID]], 1)
            v1 = jnp.concatenate([potential[:GRID, GRID:], potential[GRID:, GRID:]], 1)
            for quarter in range(4):
                s = slot_of(quarter)
                rows = slice(quarter * SLAB, (quarter + 1) * SLAB)
                x0, x1 = v0[rows], v1[rows]
                a = lead[n, s, :, lanes].astype(F32)
                b0 = own[n, s, 0, :, lanes].astype(F32)
                b1 = own[n, s, 1, :, lanes].astype(F32)
                lead[n, s, :, lanes] = ((own0 * x0) * b0 + (own1 * x1) * b1).astype(BF)
                own[n, s, 0, :, lanes] = ((lead0 * x0) * a).astype(BF)
                own[n, s, 1, :, lanes] = ((lead1 * x1) * a).astype(BF)

    def out_core(n):
        return (
            remote(own.at[n, 1], core_in.at[n, 0], send_b, recv_b, 0, 1, n, other_core),
            remote(own.at[n, 3], core_in.at[n, 1], send_b, recv_b, 1, 0, n, other_core),
        )

    def out_one(n, slot):
        far = slot // 2
        return remote(
            lead.at[n, slot],
            sums_in.at[n, far],
            send_b,
            recv_b,
            2 + slot,
            1 - flip(far, cross[-1]),
            n,
            (block(-1), 2 * flip(p, cross[-1]) + slot % 2),
        )

    def out_two(n, slot):
        far = slot // 2
        core = 1 - slot % 2
        direct = z == 2
        step = jnp.where(direct, -2, jnp.where(z == 3, -3, 1))
        chip = jnp.where(direct, flip(p, cross[-2]), p)
        index = far + jnp.where(direct, 2, 4)
        return remote(
            lead.at[n, slot],
            sums_in.at[n, index],
            send_b,
            recv_b,
            2 + slot,
            index,
            n,
            (block(step), 2 * chip + core),
        )

    out_between = z != 3

    def out_pass(n, far):
        chip = flip(p, flag((spot == 1) | (spot == 2)))
        return remote(
            sums_in.at[n, 4 + far],
            sums_in.at[n, 2 + far],
            send_b,
            recv_b,
            6 + far,
            2 + far,
            n,
            (block(jnp.where(z == 0, 1, -3)), 2 * chip + k),
        )

    def out_share(n, slot):
        return remote(
            lead.at[n, slot],
            sums_in.at[n, 7 - slot],
            send_b,
            recv_b,
            2 + slot,
            4 - 2 * slot,
            n,
            (block(-1), 2 * p),
        )

    def out_chip(n):
        return remote(own.at[n, 2], chip_in.at[n], send_b, recv_b, 8, 6, n, other_chip)

    def arrived_b(ref, sort, n):
        remote(ref, ref, send_b, recv_b, 0, sort, n, other_core).wait_recv()

    bands = [flip(p, cross[1]), flip(p, cross[2])]
    masks = [[flag(b == band).astype(F32) for b in bands] for band in range(2)]

    def lead_sums(m, far, band):
        first = sums_in[m, flip(far, cross[1])].astype(F32)
        second = sums_in[m, 2 + flip(far, cross[2])].astype(F32)
        return masks[band][0] * first + masks[band][1] * second

    def out_step(n, carry):
        @pl.when(n < CHUNKS)
        def _():
            inverse(n)

            @pl.when(k == 0)
            def _():
                out_one(n, 2).start()
                out_one(n, 3).start()

                @pl.when(jnp.logical_not(third(n)))
                def _():
                    out_one(n, 1).start()

            @pl.when(k == 1)
            def _():
                out_share(n, 1).start()
                out_two(n, 2).start()
                out_two(n, 3).start()

                @pl.when(third(n))
                def _():
                    out_share(n, 0).start()

                @pl.when(jnp.logical_not(third(n)))
                def _():
                    out_two(n, 0).start()

            for copy in out_core(n):
                copy.start()

        @pl.when((n >= OUT_LAGS[0]) & (n < CHUNKS + OUT_LAGS[0]))
        def _():
            m = n - OUT_LAGS[0]

            @pl.when(out_between)
            def _():
                arrived_b(sums_in.at[m, 5], 5, m)
                out_pass(m, 1).start()

                @pl.when((k == 1) & jnp.logical_not(third(m)))
                def _():
                    arrived_b(sums_in.at[m, 4], 4, m)
                    out_pass(m, 0).start()

        @pl.when((n >= OUT_LAGS[1]) & (n < CHUNKS + OUT_LAGS[1]))
        def _():
            m = n - OUT_LAGS[1]

            @pl.when(k == 0)
            def _():
                arrived_b(sums_in.at[m, 6], 2, m)
                total = lead[m, 0].astype(F32) + sums_in[m, 6].astype(F32)
                lead[m, 0] = total.astype(BF)
                out_one(m, 0).start()

                @pl.when(third(m))
                def _():
                    arrived_b(sums_in.at[m, 7], 4, m)
                    total = lead[m, 1].astype(F32) + sums_in[m, 7].astype(F32)
                    lead[m, 1] = total.astype(BF)
                    out_one(m, 1).start()

        @pl.when((n >= OUT_LAGS[2]) & (n < CHUNKS + OUT_LAGS[2]))
        def _():
            m = n - OUT_LAGS[2]
            arrived_b(own.at[m, 0:3, 0], 0, m)
            arrived_b(sums_in.at[m, 3], 3, m)

            @pl.when((k == 1) & jnp.logical_not(third(m)))
            def _():
                arrived_b(sums_in.at[m, 2], 2, m)

            for band in range(2):
                total = own[m, 2, band].astype(F32) + core_in[m, 1, band].astype(F32)
                own[m, 2, band] = (total + lead_sums(m, 1, band)).astype(BF)
            out_chip(m).start()

        @pl.when(n >= OUT_LAGS[3])
        def _():
            m = n - OUT_LAGS[3]
            arrived_b(own.at[m, 0:3, 0], 1, m)
            arrived_b(chip_in.at[m], 6, m)
            for band in range(2):
                total = own[m, 0, band].astype(F32) + core_in[m, 0, band].astype(F32)
                stage[m, band] = total + chip_in[m, band].astype(F32) + lead_sums(m, 0, band)
            store(m).start()

        return carry

    lax.fori_loop(0, CHUNKS + OUT_LAGS[3], out_step, 0)

    for kind, ref in enumerate((own.at[:, 0],) * 2 + (one,) * 4):
        sent(ref, send_b, kind)

    @pl.when(out_between)
    def _():
        sent(one, send_b, 7)

        @pl.when(k == 1)
        def _():
            sent(rest, send_b, 6)

    sent(own.at[:, 2], send_b, 8)
    pltpu.make_async_copy(stage, stage, store_sem.at[0]).wait()


def body(orbitals, occupation, pair_keep):
    plus, minus = tables()
    vmem = pl.BlockSpec(memory_space=pltpu.VMEM)
    smem = pl.BlockSpec(memory_space=pltpu.SMEM)
    anywhere = pl.BlockSpec(memory_space=pl.ANY)
    dma = pltpu.SemaphoreType.DMA
    return pl.pallas_call(
        kernel,
        out_shape=jax.ShapeDtypeStruct(orbitals.shape, F32),
        in_specs=[smem, smem, anywhere, vmem, vmem],
        out_specs=anywhere,
        scratch_shapes=[
            pltpu.VMEM((CHUNKS, 2, SLAB, LANES), F32),
            pltpu.VMEM((CHUNKS, 6, SLAB, LANES), BF),
            pltpu.VMEM((CHUNKS, 4, 2, SLAB, LANES), BF),
            pltpu.VMEM((TILES, 8 * GRID, GRID), F32),
            pltpu.VMEM((TILES, 8 * GRID, GRID), F32),
            pltpu.VMEM((GRID, GRID, GRID), F32),
            pltpu.VMEM((CHUNKS, 8, SLAB, LANES), BF),
            pltpu.VMEM((CHUNKS, 2, 2, SLAB, LANES), BF),
            pltpu.VMEM((CHUNKS, 2, SLAB, LANES), BF),
            pltpu.VMEM((8, GRID), F32),
            pltpu.VMEM((8, GRID), F32),
            dma((1,)),
            dma((1,)),
            dma((11,)),
            dma((5, CHUNKS)),
            dma((9,)),
            dma((7, CHUNKS)),
            dma((2,)),
        ],
        compiler_params=pltpu.CompilerParams(
            collective_id=0, has_side_effects=True, vmem_limit_bytes=62 * 1024 * 1024
        ),
        name="exchange",
    )(occupation, pair_keep, orbitals, jnp.asarray(plus), jnp.asarray(minus))


def solution(mesh):
    in_specs = (P("band", "grid", None), P("band"), P("band", None, None))
    return jax.shard_map(
        body, mesh=mesh, in_specs=in_specs, out_specs=P("band", "grid", None), check_vma=False
    )
```

```python
import functools
import math

import jax
import jax.numpy as jnp
import numpy as np
from jax import lax
from jax.experimental import pallas as pl
from jax.experimental.pallas import tpu as pltpu
from jax.sharding import PartitionSpec as P

GRID = 128
SLAB = 32
BLOCKS = 32
HALF_RING = 16
WIDTH = 64.0
CHUNKS = 16
LANES = GRID * GRID // CHUNKS
PAIRS = LANES // (2 * GRID)
TILES = GRID // 8
IN_LAGS = (3, 5, 9)
OUT_LAGS = (3, 3, 4, 6)
THIRDS = sum(n % 3 == 2 for n in range(CHUNKS))
BF = jnp.bfloat16
F32 = jnp.float32
MESH = pl.DeviceIdType.MESH


def tables():
    index = np.arange(GRID)
    angle = (index[:, None] * index[None, :] % GRID) * (2.0 * math.pi / GRID)
    cosine, sine = np.cos(angle), np.sin(angle)
    forward = np.block([[cosine, -sine], [sine, cosine]])
    return tuple(np.asarray(t, np.float32).astype(BF) for t in (forward, forward.T))


def dot(left, right):
    return jnp.dot(left, right, preferred_element_type=F32)


def regroup(value):
    n = GRID
    top = jnp.concatenate([value[:n, :n], value[n:, :n]], 1)
    low = jnp.concatenate([value[:n, n:], value[n:, n:]], 1)
    return jnp.concatenate([top, low], 0)


def kernel(
    occ, keep, orbitals, plus, minus, out,
    lead, own, real, imag, factor, sums_in, core_in, chip_in, note_out, note_in,
    load_sem, send_a, recv_a, send_b, recv_b, note_sem,
):
    c, g = lax.axis_index("band"), lax.axis_index("grid")
    p, k = lax.div(g, 2), lax.rem(g, 2)
    spot = lax.rem(c, HALF_RING)
    z = lax.rem(c, 4)

    def block(step):
        return lax.rem(c + BLOCKS + step, BLOCKS)

    def flag(condition):
        return jnp.where(condition, 1, 0)

    cross = {
        step: flag(spot >= HALF_RING - step) if step > 0 else flag(spot < -step)
        for step in (1, 2, 3, -1, -2, -3)
    }

    def flip(value, bit):
        return value + bit - 2 * value * bit

    def slot_of(quarter):
        return 2 * flip(quarter // 2, p) + flip(quarter % 2, k)

    def remote(source, target, sends, receives, kind, sort, n, device):
        return pltpu.make_async_remote_copy(
            src_ref=source,
            dst_ref=target,
            send_sem=sends.at[kind],
            recv_sem=receives.at[sort, n],
            device_id=device,
            device_id_type=MESH,
        )

    other_core = (c, 2 * p + 1 - k)
    other_chip = (c, 2 * (1 - p) + k)

    def part(n):
        return pl.ds(pl.multiple_of(n * LANES, LANES), LANES)

    def third(n):
        return lax.rem(n, 3) == 2

    def each(count, step):
        def run(n, carry):
            step(n)
            return carry

        lax.fori_loop(0, count, run, 0)

    barrier = pltpu.get_barrier_semaphore()

    def greet(band, grid):
        pl.semaphore_signal(barrier, inc=1, device_id=(band, grid), device_id_type=MESH)

    for step in (1, -1):

        @pl.when(cross[step] == 1)
        def _(step=step):
            for core in (0, 1):
                greet(block(step), 2 * (1 - p) + core)

    for step in (3, -3, 1, -1, 2, -2):
        for core in (0, 1):
            greet(block(step), 2 * (flip(p, cross[step]) if abs(step) == 3 else p) + core)
    greet(*other_core)
    greet(*other_chip)

    fetch = pltpu.make_async_copy(orbitals, out, load_sem.at[0])
    fetch.start()

    def clear(n):
        @pl.when((k == 0) | third(n))
        def _():
            sums_in[n, 2] = jnp.zeros((SLAB, LANES), BF)

    each(CHUNKS, clear)
    note_out[...] = jnp.zeros((8, GRID), F32) + occ[p]
    fetch.wait()
    own[0, 0] = out[:, :, part(0)].astype(BF)
    pl.semaphore_wait(barrier, 14 + 2 * (cross[1] + cross[-1]))

    note = pltpu.make_async_remote_copy(
        src_ref=note_out,
        dst_ref=note_in,
        send_sem=note_sem.at[0],
        recv_sem=note_sem.at[1],
        device_id=(lax.rem(c + 1 + k, BLOCKS), g),
        device_id_type=MESH,
    )
    note.start()

    def in_bands(n):
        mine = own.at[n, 0]
        return (
            remote(mine, own.at[n, 2], send_a, recv_a, 0, 0, n, other_chip),
            remote(mine, own.at[n, 1], send_a, recv_a, 1, 1, n, other_core),
        )

    def in_core(n):
        return remote(own.at[n, 2], own.at[n, 3], send_a, recv_a, 4, 1, n, other_core)

    def in_one(n, far):
        chip = flip(p, cross[1])
        return remote(
            own.at[n, 2 * flip(far, cross[1]), chip],
            lead.at[n, k + 2 * far],
            send_a,
            recv_a,
            2 + far,
            2 - far,
            n,
            (block(1), 2 * chip),
        )

    def in_two(n, far):
        chip = flip(p, cross[2])
        direct = z == 1
        step = jnp.where(direct, 2, jnp.where(z == 0, 3, -1))
        device = jnp.where(direct, 2 * chip + 1, g)
        return remote(
            own.at[n, 2 * flip(far, cross[2]), chip],
            lead.at[n, jnp.where(direct, 1 - k + 2 * far, 4 + far)],
            send_a,
            recv_a,
            5 + far,
            jnp.where(direct, 2 - far, 3 + far),
            n,
            (block(step), device),
        )

    in_between = z != 0

    def in_pass(n, far):
        chip = flip(p, flag((spot == HALF_RING - 3) | (spot == HALF_RING - 2)))
        return remote(
            lead.at[n, 4 + far],
            lead.at[n, 1 - k + 2 * far],
            send_a,
            recv_a,
            7 + far,
            2 - far,
            n,
            (block(jnp.where(z == 3, -1, 3)), 2 * chip + 1),
        )

    def in_share(n, slot):
        return remote(
            lead.at[n, slot],
            lead.at[n, 1 - slot],
            send_a,
            recv_a,
            9 + slot,
            2,
            n,
            (block(1), 2 * p + 1),
        )

    def in_leads(n, second):
        in_one(n, flip(second, cross[1])).start()
        far = flip(second, cross[2])

        @pl.when((far == 1) | ((k == 1) & jnp.logical_not(third(n))))
        def _():
            in_two(n, far).start()

    def sent(ref, sends, kind):
        pltpu.make_async_remote_copy(
            src_ref=ref,
            dst_ref=ref,
            send_sem=sends.at[kind],
            recv_sem=note_sem.at[1],
            device_id=other_core,
            device_id_type=MESH,
        ).wait_send()

    def arrived_a(ref, sort, n):
        remote(ref, ref, send_a, recv_a, 0, sort, n, other_core).wait_recv()

    def make_factor(n):
        shape = (GRID, GRID)
        rows = lax.broadcasted_iota(jnp.int32, shape, 0)
        columns = lax.broadcasted_iota(jnp.int32, shape, 1)

        def squared(index):
            freq = jnp.where(index >= GRID // 2, index - GRID, index).astype(F32)
            return freq * freq

        base = squared(rows) + squared(columns)

        def plane(i, carry):
            kx = n * (GRID // CHUNKS) + i
            q = (base + squared(jnp.full(shape, kx, jnp.int32))) * (1.0 / WIDTH)
            safe = jnp.where(q > 0, q, 1.0)
            ratio = jnp.where(q > 0, (1.0 - jnp.exp(-safe)) / safe, 1.0)
            factor[kx] = ratio * (4.0 / GRID**3)
            return carry

        lax.fori_loop(0, GRID // CHUNKS, plane, 0)

    def rows_of(y):
        return pl.ds(pl.multiple_of(y * 8, 8), 8)

    def forward(n):
        for pair in range(PAIRS):
            lanes = slice(pair * 2 * GRID, (pair + 1) * 2 * GRID)
            slots = [slot_of(quarter) for quarter in range(4)]
            first = jnp.concatenate([lead[n, s, :, lanes] for s in slots], 0)
            parts = [
                first * jnp.concatenate([own[n, s, j, :, lanes] for s in slots], 0)
                for j in range(2)
            ]
            mixed = regroup(dot(minus[...], jnp.concatenate(parts, 0)).astype(BF))
            result = dot(mixed, plus[...])
            for half in range(2):
                rows = rows_of(n * 2 * PAIRS + 2 * pair + half)
                for t in range(TILES):
                    at = half * GRID + t * 8
                    real[t, rows, :] = result[at : at + 8, :GRID]
                    imag[t, rows, :] = result[at : at + 8, GRID:]

    def in_step(n, carry):
        @pl.when(n < CHUNKS)
        def _():
            for copy in in_bands(n):
                copy.start()
            in_leads(n, 0)
            later = jnp.minimum(n + 1, CHUNKS - 1)

            @pl.when(later > n)
            def _():
                own[later, 0] = out[:, :, part(later)].astype(BF)

            make_factor(n)

        @pl.when((n >= IN_LAGS[0]) & (n < CHUNKS + IN_LAGS[0]))
        def _():
            m = n - IN_LAGS[0]
            arrived_a(own.at[m, 2], 0, m)
            in_leads(m, 1)
            in_core(m).start()

        @pl.when((n >= IN_LAGS[1]) & (n < CHUNKS + IN_LAGS[1]))
        def _():
            m = n - IN_LAGS[1]

            @pl.when(in_between)
            def _():
                arrived_a(lead.at[m, 5], 4, m)
                in_pass(m, 1).start()

                @pl.when((k == 1) & jnp.logical_not(third(m)))
                def _():
                    arrived_a(lead.at[m, 4], 3, m)
                    in_pass(m, 0).start()

            @pl.when(k == 0)
            def _():
                arrived_a(lead.at[m, 0:2], 2, m)
                in_share(m, 0).start()

                @pl.when(third(m))
                def _():
                    in_share(m, 1).start()

        @pl.when(n >= IN_LAGS[2])
        def _():
            m = n - IN_LAGS[2]

            @pl.when(k == 1)
            def _():
                arrived_a(lead.at[m, 0:2], 2, m)

            arrived_a(own.at[m, 0:3], 1, m)
            forward(m)

        return carry

    lax.fori_loop(0, CHUNKS + IN_LAGS[2], in_step, 0)

    def middle(step):
        for t in (8 * step + i for i in range(8)):
            for pair in range(4):
                pick = [pl.ds(2 * pair + half, GRID, stride=8) for half in range(2)]
                packed = jnp.concatenate(
                    [jnp.concatenate([w[t, r, :] for r in pick], 1) for w in (real, imag)], 0
                ).astype(BF)
                scale = jnp.concatenate(
                    [factor[t * 8 + 2 * pair], factor[t * 8 + 2 * pair + 1]], 1
                )
                scale = jnp.concatenate([scale, scale], 0)
                field = (dot(minus[...], packed) * scale).astype(BF)
                result = dot(plus[...], field)
                for half in range(2):
                    at = slice(half * GRID, (half + 1) * GRID)
                    real[t, pick[half], :] = result[:GRID, at]
                    imag[t, pick[half], :] = result[GRID:, at]

    each(TILES // 8, middle)

    one, some, rest = lead.at[:, 0], lead.at[:THIRDS, 0], lead.at[THIRDS:, 0]
    for kind, ref in enumerate((own.at[:, 0], own.at[:, 0], one, one, own.at[:, 2])):
        sent(ref, send_a, kind)
    sent(one, send_a, 6)

    @pl.when(k == 1)
    def _():
        sent(rest, send_a, 5)

    @pl.when(k == 0)
    def _():
        sent(one, send_a, 9)
        sent(some, send_a, 10)

    @pl.when(in_between)
    def _():
        sent(one, send_a, 8)

        @pl.when(k == 1)
        def _():
            sent(rest, send_a, 7)

    note.wait()
    kept = [keep[j, k, p].astype(F32) for j in range(2)]
    own0, own1 = (-(occ[j] * kept[j]) for j in range(2))
    amount = jnp.concatenate([note_in[0:1, :]] * 2, 1)
    lead0, lead1 = (-(amount * kept[j]) for j in range(2))

    def inverse(n):
        for pair in range(PAIRS):
            lanes = slice(pair * 2 * GRID, (pair + 1) * 2 * GRID)

            def field(w):
                halves = []
                for half in range(2):
                    rows = rows_of(n * 2 * PAIRS + 2 * pair + half)
                    halves.append(jnp.concatenate([w[t, rows, :] for t in range(TILES)], 0))
                return jnp.concatenate(halves, 1)

            packed = jnp.concatenate([field(real), field(imag)], 0).astype(BF)
            mixed = regroup(dot(plus[...], packed).astype(BF))
            potential = dot(mixed, minus[...])
            v0 = jnp.concatenate([potential[:GRID, :GRID], potential[GRID:, :GRID]], 1)
            v1 = jnp.concatenate([potential[:GRID, GRID:], potential[GRID:, GRID:]], 1)
            for quarter in range(4):
                s = slot_of(quarter)
                rows = slice(quarter * SLAB, (quarter + 1) * SLAB)
                x0, x1 = v0[rows], v1[rows]
                a = lead[n, s, :, lanes].astype(F32)
                b0 = own[n, s, 0, :, lanes].astype(F32)
                b1 = own[n, s, 1, :, lanes].astype(F32)
                lead[n, s, :, lanes] = ((own0 * x0) * b0 + (own1 * x1) * b1).astype(BF)
                own[n, s, 0, :, lanes] = ((lead0 * x0) * a).astype(BF)
                own[n, s, 1, :, lanes] = ((lead1 * x1) * a).astype(BF)

    def out_core(n):
        return (
            remote(own.at[n, 1], core_in.at[n, 0], send_b, recv_b, 0, 1, n, other_core),
            remote(own.at[n, 3], core_in.at[n, 1], send_b, recv_b, 1, 0, n, other_core),
        )

    def out_one(n, slot):
        far = slot // 2
        return remote(
            lead.at[n, slot],
            sums_in.at[n, far],
            send_b,
            recv_b,
            2 + slot,
            1 - flip(far, cross[-1]),
            n,
            (block(-1), 2 * flip(p, cross[-1]) + slot % 2),
        )

    def out_two(n, slot):
        far = slot // 2
        core = 1 - slot % 2
        direct = z == 2
        step = jnp.where(direct, -2, jnp.where(z == 3, -3, 1))
        chip = jnp.where(direct, flip(p, cross[-2]), p)
        index = far + jnp.where(direct, 2, 4)
        return remote(
            lead.at[n, slot],
            sums_in.at[n, index],
            send_b,
            recv_b,
            2 + slot,
            index,
            n,
            (block(step), 2 * chip + core),
        )

    out_between = z != 3

    def out_pass(n, far):
        chip = flip(p, flag((spot == 1) | (spot == 2)))
        return remote(
            sums_in.at[n, 4 + far],
            sums_in.at[n, 2 + far],
            send_b,
            recv_b,
            6 + far,
            2 + far,
            n,
            (block(jnp.where(z == 0, 1, -3)), 2 * chip + k),
        )

    def out_share(n, slot):
        return remote(
            lead.at[n, slot],
            sums_in.at[n, 7 - slot],
            send_b,
            recv_b,
            2 + slot,
            4 - 2 * slot,
            n,
            (block(-1), 2 * p),
        )

    def out_chip(n):
        return remote(own.at[n, 2], chip_in.at[n], send_b, recv_b, 8, 6, n, other_chip)

    def arrived_b(ref, sort, n):
        remote(ref, ref, send_b, recv_b, 0, sort, n, other_core).wait_recv()

    bands = [flip(p, cross[1]), flip(p, cross[2])]
    masks = [[flag(b == band).astype(F32) for b in bands] for band in range(2)]

    def lead_sums(m, far, band):
        first = sums_in[m, flip(far, cross[1])].astype(F32)
        second = sums_in[m, 2 + flip(far, cross[2])].astype(F32)
        return masks[band][0] * first + masks[band][1] * second

    def out_step(n, carry):
        @pl.when(n < CHUNKS)
        def _():
            inverse(n)

            @pl.when(k == 0)
            def _():
                out_one(n, 2).start()
                out_one(n, 3).start()

                @pl.when(jnp.logical_not(third(n)))
                def _():
                    out_one(n, 1).start()

            @pl.when(k == 1)
            def _():
                out_share(n, 1).start()
                out_two(n, 2).start()
                out_two(n, 3).start()

                @pl.when(third(n))
                def _():
                    out_share(n, 0).start()

                @pl.when(jnp.logical_not(third(n)))
                def _():
                    out_two(n, 0).start()

            for copy in out_core(n):
                copy.start()

        @pl.when((n >= OUT_LAGS[0]) & (n < CHUNKS + OUT_LAGS[0]))
        def _():
            m = n - OUT_LAGS[0]

            @pl.when(out_between)
            def _():
                arrived_b(sums_in.at[m, 5], 5, m)
                out_pass(m, 1).start()

                @pl.when((k == 1) & jnp.logical_not(third(m)))
                def _():
                    arrived_b(sums_in.at[m, 4], 4, m)
                    out_pass(m, 0).start()

        @pl.when((n >= OUT_LAGS[1]) & (n < CHUNKS + OUT_LAGS[1]))
        def _():
            m = n - OUT_LAGS[1]

            @pl.when(k == 0)
            def _():
                arrived_b(sums_in.at[m, 6], 2, m)
                total = lead[m, 0].astype(F32) + sums_in[m, 6].astype(F32)
                lead[m, 0] = total.astype(BF)
                out_one(m, 0).start()

                @pl.when(third(m))
                def _():
                    arrived_b(sums_in.at[m, 7], 4, m)
                    total = lead[m, 1].astype(F32) + sums_in[m, 7].astype(F32)
                    lead[m, 1] = total.astype(BF)
                    out_one(m, 1).start()

        @pl.when((n >= OUT_LAGS[2]) & (n < CHUNKS + OUT_LAGS[2]))
        def _():
            m = n - OUT_LAGS[2]
            arrived_b(own.at[m, 0:3, 0], 0, m)
            arrived_b(sums_in.at[m, 3], 3, m)

            @pl.when((k == 1) & jnp.logical_not(third(m)))
            def _():
                arrived_b(sums_in.at[m, 2], 2, m)

            for band in range(2):
                total = own[m, 2, band].astype(F32) + core_in[m, 1, band].astype(F32)
                own[m, 2, band] = (total + lead_sums(m, 1, band)).astype(BF)
            out_chip(m).start()

        @pl.when(n >= OUT_LAGS[3])
        def _():
            m = n - OUT_LAGS[3]
            arrived_b(own.at[m, 0:3, 0], 1, m)
            arrived_b(chip_in.at[m], 6, m)
            for band in range(2):
                total = own[m, 0, band].astype(F32) + core_in[m, 0, band].astype(F32)
                out[band, :, part(m)] = (
                    total + chip_in[m, band].astype(F32) + lead_sums(m, 0, band)
                )

        return carry

    lax.fori_loop(0, CHUNKS + OUT_LAGS[3], out_step, 0)

    for kind, ref in enumerate((own.at[:, 0],) * 2 + (one,) * 4):
        sent(ref, send_b, kind)

    @pl.when(out_between)
    def _():
        sent(one, send_b, 7)

        @pl.when(k == 1)
        def _():
            sent(rest, send_b, 6)

    sent(own.at[:, 2], send_b, 8)


def body(orbitals, occupation, pair_keep):
    plus, minus = tables()
    vmem = pl.BlockSpec(memory_space=pltpu.VMEM)
    smem = pl.BlockSpec(memory_space=pltpu.SMEM)
    anywhere = pl.BlockSpec(memory_space=pl.ANY)
    dma = pltpu.SemaphoreType.DMA
    return pl.pallas_call(
        kernel,
        out_shape=pltpu.VMEM(orbitals.shape, F32),
        in_specs=[smem, smem, anywhere, vmem, vmem],
        out_specs=vmem,
        scratch_shapes=[
            pltpu.VMEM((CHUNKS, 6, SLAB, LANES), BF),
            pltpu.VMEM((CHUNKS, 4, 2, SLAB, LANES), BF),
            pltpu.VMEM((TILES, 8 * GRID, GRID), F32),
            pltpu.VMEM((TILES, 8 * GRID, GRID), F32),
            pltpu.VMEM((GRID, GRID, GRID), F32),
            pltpu.VMEM((CHUNKS, 8, SLAB, LANES), BF),
            pltpu.VMEM((CHUNKS, 2, 2, SLAB, LANES), BF),
            pltpu.VMEM((CHUNKS, 2, SLAB, LANES), BF),
            pltpu.VMEM((8, GRID), F32),
            pltpu.VMEM((8, GRID), F32),
            dma((1,)),
            dma((11,)),
            dma((5, CHUNKS)),
            dma((9,)),
            dma((7, CHUNKS)),
            dma((2,)),
        ],
        compiler_params=pltpu.CompilerParams(
            collective_id=0, has_side_effects=True, vmem_limit_bytes=58 * 1024 * 1024
        ),
        name="exchange",
    )(occupation, pair_keep, orbitals, jnp.asarray(plus), jnp.asarray(minus))


def solution(mesh):
    in_specs = (P("band", "grid", None), P("band"), P("band", None, None))
    return jax.shard_map(
        body, mesh=mesh, in_specs=in_specs, out_specs=P("band", "grid", None), check_vma=False
    )
```

```python
import functools
import math

import jax
import jax.numpy as jnp
import numpy as np
from jax import lax
from jax.experimental import pallas as pl
from jax.experimental.pallas import tpu as pltpu
from jax.sharding import PartitionSpec as P

GRID = 128
SLAB = 32
BLOCKS = 32
HALF_RING = 16
WIDTH = 64.0
CHUNKS = 16
LANES = GRID * GRID // CHUNKS
PAIRS = LANES // (2 * GRID)
TILES = GRID // 8
IN_LAGS = (4, 6, 10)
OUT_LAGS = (3, 3, 4, 6)
THIRDS = CHUNKS // 3
BF = jnp.bfloat16
F32 = jnp.float32
MESH = pl.DeviceIdType.MESH


def tables():
    index = np.arange(GRID)
    angle = (index[:, None] * index[None, :] % GRID) * (2.0 * math.pi / GRID)
    cosine, sine = np.cos(angle), np.sin(angle)
    forward = np.block([[cosine, -sine], [sine, cosine]])
    return tuple(np.asarray(t, np.float32).astype(BF) for t in (forward, forward.T))


def dot(left, right):
    return jnp.dot(left, right, preferred_element_type=F32)


def regroup(value):
    n = GRID
    top = jnp.concatenate([value[:n, :n], value[n:, :n]], 1)
    low = jnp.concatenate([value[:n, n:], value[n:, n:]], 1)
    return jnp.concatenate([top, low], 0)


def kernel(
    occ, keep, orbitals, plus, minus, out,
    lead, own, real, imag, factor, sums_in, core_in, chip_in, note_out, note_in,
    load_sem, send_a, recv_a, send_b, recv_b, note_sem,
):
    c, g = lax.axis_index("band"), lax.axis_index("grid")
    p, k = lax.div(g, 2), lax.rem(g, 2)
    spot = lax.rem(c, HALF_RING)
    z = lax.rem(c, 4)

    def block(step):
        return lax.rem(c + BLOCKS + step, BLOCKS)

    def flag(condition):
        return jnp.where(condition, 1, 0)

    cross = {
        step: flag(spot >= HALF_RING - step) if step > 0 else flag(spot < -step)
        for step in (1, 2, 3, -1, -2, -3)
    }

    def flip(value, bit):
        return value + bit - 2 * value * bit

    def slot_of(quarter):
        return 2 * flip(quarter // 2, p) + flip(quarter % 2, k)

    def remote(source, target, sends, receives, kind, sort, n, device):
        return pltpu.make_async_remote_copy(
            src_ref=source,
            dst_ref=target,
            send_sem=sends.at[kind],
            recv_sem=receives.at[sort, n],
            device_id=device,
            device_id_type=MESH,
        )

    other_core = (c, 2 * p + 1 - k)
    other_chip = (c, 2 * (1 - p) + k)

    def part(n):
        return pl.ds(pl.multiple_of(n * LANES, LANES), LANES)

    def third(n):
        return (lax.rem(n, 2) == 0) & (n < 2 * THIRDS)

    def each(count, step):
        def run(n, carry):
            step(n)
            return carry

        lax.fori_loop(0, count, run, 0)

    barrier = pltpu.get_barrier_semaphore()

    def greet(band, grid):
        pl.semaphore_signal(barrier, inc=1, device_id=(band, grid), device_id_type=MESH)

    for step in (1, -1):

        @pl.when(cross[step] == 1)
        def _(step=step):
            for core in (0, 1):
                greet(block(step), 2 * (1 - p) + core)

    for step in (3, -3, 1, -1, 2, -2):
        for core in (0, 1):
            greet(block(step), 2 * (flip(p, cross[step]) if abs(step) == 3 else p) + core)
    greet(*other_core)
    greet(*other_chip)

    fetch = pltpu.make_async_copy(orbitals, out, load_sem.at[0])
    fetch.start()

    def clear(n):
        @pl.when((k == 0) | third(n))
        def _():
            sums_in[n, 2] = jnp.zeros((SLAB, LANES), BF)

    each(CHUNKS, clear)
    note_out[...] = jnp.zeros((8, GRID), F32) + occ[p]
    fetch.wait()
    own[0, 0] = out[:, :, part(0)].astype(BF)
    pl.semaphore_wait(barrier, 14 + 2 * (cross[1] + cross[-1]))

    note = pltpu.make_async_remote_copy(
        src_ref=note_out,
        dst_ref=note_in,
        send_sem=note_sem.at[0],
        recv_sem=note_sem.at[1],
        device_id=(lax.rem(c + 1 + k, BLOCKS), g),
        device_id_type=MESH,
    )
    note.start()

    def in_bands(n):
        mine = own.at[n, 0]
        return (
            remote(mine, own.at[n, 2], send_a, recv_a, 0, 0, n, other_chip),
            remote(mine, own.at[n, 1], send_a, recv_a, 1, 1, n, other_core),
        )

    def in_core(n):
        return remote(own.at[n, 2], own.at[n, 3], send_a, recv_a, 4, 1, n, other_core)

    def in_one(n, far):
        chip = flip(p, cross[1])
        return remote(
            own.at[n, 2 * flip(far, cross[1]), chip],
            lead.at[n, k + 2 * far],
            send_a,
            recv_a,
            2 + far,
            2 - far,
            n,
            (block(1), 2 * chip),
        )

    def in_two(n, far):
        chip = flip(p, cross[2])
        direct = z == 1
        step = jnp.where(direct, 2, jnp.where(z == 0, 3, -1))
        device = jnp.where(direct, 2 * chip + 1, g)
        return remote(
            own.at[n, 2 * flip(far, cross[2]), chip],
            lead.at[n, jnp.where(direct, 1 - k + 2 * far, 4 + far)],
            send_a,
            recv_a,
            5 + far,
            jnp.where(direct, 2 - far, 3),
            n,
            (block(step), device),
        )

    in_between = z != 0

    def in_pass(n, far):
        chip = flip(p, flag((spot == HALF_RING - 3) | (spot == HALF_RING - 2)))
        return remote(
            lead.at[n, 4 + far],
            lead.at[n, 1 - k + 2 * far],
            send_a,
            recv_a,
            7 + far,
            2 - far,
            n,
            (block(jnp.where(z == 3, -1, 3)), 2 * chip + 1),
        )

    def in_share(n, slot):
        return remote(
            lead.at[n, slot],
            lead.at[n, 1 - slot],
            send_a,
            recv_a,
            9 + slot,
            2,
            n,
            (block(1), 2 * p + 1),
        )

    def in_leads(n, second):
        in_one(n, flip(second, cross[1])).start()
        far = flip(second, cross[2])

        @pl.when((far == 1) | ((k == 1) & jnp.logical_not(third(n))))
        def _():
            in_two(n, far).start()

    def sent(ref, sends, kind):
        pltpu.make_async_remote_copy(
            src_ref=ref,
            dst_ref=ref,
            send_sem=sends.at[kind],
            recv_sem=note_sem.at[1],
            device_id=other_core,
            device_id_type=MESH,
        ).wait_send()

    def arrived_a(ref, sort, n):
        remote(ref, ref, send_a, recv_a, 0, sort, n, other_core).wait_recv()

    def make_factor(n):
        shape = (GRID, GRID)
        rows = lax.broadcasted_iota(jnp.int32, shape, 0)
        columns = lax.broadcasted_iota(jnp.int32, shape, 1)

        def squared(index):
            freq = jnp.where(index >= GRID // 2, index - GRID, index).astype(F32)
            return freq * freq

        base = squared(rows) + squared(columns)

        def plane(i, carry):
            kx = n * (GRID // CHUNKS) + i
            q = (base + squared(jnp.full(shape, kx, jnp.int32))) * (1.0 / WIDTH)
            safe = jnp.where(q > 0, q, 1.0)
            ratio = jnp.where(q > 0, (1.0 - jnp.exp(-safe)) / safe, 1.0)
            factor[kx] = ratio * (4.0 / GRID**3)
            return carry

        lax.fori_loop(0, GRID // CHUNKS, plane, 0)

    def rows_of(y):
        return pl.ds(pl.multiple_of(y * 8, 8), 8)

    def forward(n):
        for pair in range(PAIRS):
            lanes = slice(pair * 2 * GRID, (pair + 1) * 2 * GRID)
            slots = [slot_of(quarter) for quarter in range(4)]
            first = jnp.concatenate([lead[n, s, :, lanes] for s in slots], 0)
            parts = [
                first * jnp.concatenate([own[n, s, j, :, lanes] for s in slots], 0)
                for j in range(2)
            ]
            mixed = regroup(dot(minus[...], jnp.concatenate(parts, 0)).astype(BF))
            result = dot(mixed, plus[...])
            for half in range(2):
                rows = rows_of(n * 2 * PAIRS + 2 * pair + half)
                for t in range(TILES):
                    at = half * GRID + t * 8
                    real[t, rows, :] = result[at : at + 8, :GRID]
                    imag[t, rows, :] = result[at : at + 8, GRID:]

    def in_step(n, carry):
        @pl.when(n < CHUNKS)
        def _():
            for copy in in_bands(n):
                copy.start()
            in_leads(n, 0)
            later = jnp.minimum(n + 1, CHUNKS - 1)

            @pl.when(later > n)
            def _():
                own[later, 0] = out[:, :, part(later)].astype(BF)

            make_factor(n)

        @pl.when((n >= IN_LAGS[0]) & (n < CHUNKS + IN_LAGS[0]))
        def _():
            m = n - IN_LAGS[0]
            arrived_a(own.at[m, 2], 0, m)
            in_leads(m, 1)
            in_core(m).start()

        @pl.when((n >= IN_LAGS[1]) & (n < CHUNKS + IN_LAGS[1]))
        def _():
            m = n - IN_LAGS[1]

            @pl.when(in_between)
            def _():
                both = (k == 1) & jnp.logical_not(third(m))

                @pl.when(both)
                def _():
                    arrived_a(lead.at[m, 4:6], 3, m)
                    in_pass(m, 0).start()

                @pl.when(jnp.logical_not(both))
                def _():
                    arrived_a(lead.at[m, 5], 3, m)

                in_pass(m, 1).start()

            @pl.when(k == 0)
            def _():
                arrived_a(lead.at[m, 0:2], 2, m)
                in_share(m, 0).start()

                @pl.when(third(m))
                def _():
                    in_share(m, 1).start()

        @pl.when(n >= IN_LAGS[2])
        def _():
            m = n - IN_LAGS[2]

            @pl.when(k == 1)
            def _():
                arrived_a(lead.at[m, 0:2], 2, m)

            arrived_a(own.at[m, 0:3], 1, m)
            forward(m)

        return carry

    lax.fori_loop(0, CHUNKS + IN_LAGS[2], in_step, 0)

    def middle(step):
        for t in (8 * step + i for i in range(8)):
            for pair in range(4):
                pick = [pl.ds(2 * pair + half, GRID, stride=8) for half in range(2)]
                packed = jnp.concatenate(
                    [jnp.concatenate([w[t, r, :] for r in pick], 1) for w in (real, imag)], 0
                ).astype(BF)
                scale = jnp.concatenate(
                    [factor[t * 8 + 2 * pair], factor[t * 8 + 2 * pair + 1]], 1
                )
                scale = jnp.concatenate([scale, scale], 0)
                field = (dot(minus[...], packed) * scale).astype(BF)
                result = dot(plus[...], field)
                for half in range(2):
                    at = slice(half * GRID, (half + 1) * GRID)
                    real[t, pick[half], :] = result[:GRID, at]
                    imag[t, pick[half], :] = result[GRID:, at]

    each(TILES // 8, middle)

    one, some, rest = lead.at[:, 0], lead.at[:THIRDS, 0], lead.at[THIRDS:, 0]
    for kind, ref in enumerate((own.at[:, 0], own.at[:, 0], one, one, own.at[:, 2])):
        sent(ref, send_a, kind)
    sent(one, send_a, 6)

    @pl.when(k == 1)
    def _():
        sent(rest, send_a, 5)

    @pl.when(k == 0)
    def _():
        sent(one, send_a, 9)
        sent(some, send_a, 10)

    @pl.when(in_between)
    def _():
        sent(one, send_a, 8)

        @pl.when(k == 1)
        def _():
            sent(rest, send_a, 7)

    note.wait()
    kept = [keep[j, k, p].astype(F32) for j in range(2)]
    own0, own1 = (-(occ[j] * kept[j]) for j in range(2))
    amount = jnp.concatenate([note_in[0:1, :]] * 2, 1)
    lead0, lead1 = (-(amount * kept[j]) for j in range(2))

    def inverse(n):
        for pair in range(PAIRS):
            lanes = slice(pair * 2 * GRID, (pair + 1) * 2 * GRID)

            def field(w):
                halves = []
                for half in range(2):
                    rows = rows_of(n * 2 * PAIRS + 2 * pair + half)
                    halves.append(jnp.concatenate([w[t, rows, :] for t in range(TILES)], 0))
                return jnp.concatenate(halves, 1)

            packed = jnp.concatenate([field(real), field(imag)], 0).astype(BF)
            mixed = regroup(dot(plus[...], packed).astype(BF))
            potential = dot(mixed, minus[...])
            v0 = jnp.concatenate([potential[:GRID, :GRID], potential[GRID:, :GRID]], 1)
            v1 = jnp.concatenate([potential[:GRID, GRID:], potential[GRID:, GRID:]], 1)
            for quarter in range(4):
                s = slot_of(quarter)
                rows = slice(quarter * SLAB, (quarter + 1) * SLAB)
                x0, x1 = v0[rows], v1[rows]
                a = lead[n, s, :, lanes].astype(F32)
                b0 = own[n, s, 0, :, lanes].astype(F32)
                b1 = own[n, s, 1, :, lanes].astype(F32)
                lead[n, s, :, lanes] = ((own0 * x0) * b0 + (own1 * x1) * b1).astype(BF)
                own[n, s, 0, :, lanes] = ((lead0 * x0) * a).astype(BF)
                own[n, s, 1, :, lanes] = ((lead1 * x1) * a).astype(BF)

    def out_core(n):
        return (
            remote(own.at[n, 1], core_in.at[n, 0], send_b, recv_b, 0, 1, n, other_core),
            remote(own.at[n, 3], core_in.at[n, 1], send_b, recv_b, 1, 0, n, other_core),
        )

    def out_one(n, slot):
        far = slot // 2
        return remote(
            lead.at[n, slot],
            sums_in.at[n, far],
            send_b,
            recv_b,
            2 + slot,
            1 - flip(far, cross[-1]),
            n,
            (block(-1), 2 * flip(p, cross[-1]) + slot % 2),
        )

    def out_two(n, slot):
        far = slot // 2
        core = 1 - slot % 2
        direct = z == 2
        step = jnp.where(direct, -2, jnp.where(z == 3, -3, 1))
        chip = jnp.where(direct, flip(p, cross[-2]), p)
        index = far + jnp.where(direct, 2, 4)
        return remote(
            lead.at[n, slot],
            sums_in.at[n, index],
            send_b,
            recv_b,
            2 + slot,
            jnp.where(direct, 2 - 2 * far, 3 + far),
            n,
            (block(step), 2 * chip + core),
        )

    out_between = z != 3

    def out_pass(n, far):
        chip = flip(p, flag((spot == 1) | (spot == 2)))
        return remote(
            sums_in.at[n, 4 + far],
            sums_in.at[n, 2 + far],
            send_b,
            recv_b,
            6 + far,
            2 - 2 * far,
            n,
            (block(jnp.where(z == 0, 1, -3)), 2 * chip + k),
        )

    def out_share(n, slot):
        return remote(
            lead.at[n, slot],
            sums_in.at[n, 7 - slot],
            send_b,
            recv_b,
            2 + slot,
            3 - slot,
            n,
            (block(-1), 2 * p),
        )

    def out_chip(n):
        return remote(own.at[n, 2], chip_in.at[n], send_b, recv_b, 8, 1, n, other_chip)

    def arrived_b(ref, sort, n):
        remote(ref, ref, send_b, recv_b, 0, sort, n, other_core).wait_recv()

    bands = [flip(p, cross[1]), flip(p, cross[2])]
    masks = [[flag(b == band).astype(F32) for b in bands] for band in range(2)]

    def lead_sums(m, far, band):
        first = sums_in[m, flip(far, cross[1])].astype(F32)
        second = sums_in[m, 2 + flip(far, cross[2])].astype(F32)
        return masks[band][0] * first + masks[band][1] * second

    def out_step(n, carry):
        @pl.when(n < CHUNKS)
        def _():
            inverse(n)

            @pl.when(k == 0)
            def _():
                out_one(n, 2).start()
                out_one(n, 3).start()

                @pl.when(jnp.logical_not(third(n)))
                def _():
                    out_one(n, 1).start()

            @pl.when(k == 1)
            def _():
                out_share(n, 1).start()
                out_two(n, 2).start()
                out_two(n, 3).start()

                @pl.when(third(n))
                def _():
                    out_share(n, 0).start()

                @pl.when(jnp.logical_not(third(n)))
                def _():
                    out_two(n, 0).start()

            for copy in out_core(n):
                copy.start()

        @pl.when((n >= OUT_LAGS[0]) & (n < CHUNKS + OUT_LAGS[0]))
        def _():
            m = n - OUT_LAGS[0]

            @pl.when(out_between)
            def _():
                arrived_b(sums_in.at[m, 5], 4, m)
                out_pass(m, 1).start()

                @pl.when((k == 1) & jnp.logical_not(third(m)))
                def _():
                    arrived_b(sums_in.at[m, 4], 3, m)
                    out_pass(m, 0).start()

        @pl.when((n >= OUT_LAGS[1]) & (n < CHUNKS + OUT_LAGS[1]))
        def _():
            m = n - OUT_LAGS[1]

            @pl.when(k == 0)
            def _():
                arrived_b(sums_in.at[m, 6], 2, m)
                total = lead[m, 0].astype(F32) + sums_in[m, 6].astype(F32)
                lead[m, 0] = total.astype(BF)
                out_one(m, 0).start()

                @pl.when(third(m))
                def _():
                    arrived_b(sums_in.at[m, 7], 3, m)
                    total = lead[m, 1].astype(F32) + sums_in[m, 7].astype(F32)
                    lead[m, 1] = total.astype(BF)
                    out_one(m, 1).start()

        @pl.when((n >= OUT_LAGS[2]) & (n < CHUNKS + OUT_LAGS[2]))
        def _():
            m = n - OUT_LAGS[2]
            arrived_b(sums_in.at[m, 0:4], 0, m)

            @pl.when((k == 1) & jnp.logical_not(third(m)))
            def _():
                arrived_b(sums_in.at[m, 2], 2, m)

            for band in range(2):
                total = own[m, 2, band].astype(F32) + core_in[m, 1, band].astype(F32)
                own[m, 2, band] = (total + lead_sums(m, 1, band)).astype(BF)
            out_chip(m).start()

        @pl.when(n >= OUT_LAGS[3])
        def _():
            m = n - OUT_LAGS[3]
            arrived_b(sums_in.at[m, 0:5], 1, m)
            for band in range(2):
                total = own[m, 0, band].astype(F32) + core_in[m, 0, band].astype(F32)
                out[band, :, part(m)] = (
                    total + chip_in[m, band].astype(F32) + lead_sums(m, 0, band)
                )

        return carry

    lax.fori_loop(0, CHUNKS + OUT_LAGS[3], out_step, 0)

    for kind, ref in enumerate((own.at[:, 0],) * 2 + (one,) * 4):
        sent(ref, send_b, kind)

    @pl.when(out_between)
    def _():
        sent(one, send_b, 7)

        @pl.when(k == 1)
        def _():
            sent(rest, send_b, 6)

    sent(own.at[:, 2], send_b, 8)


def body(orbitals, occupation, pair_keep):
    plus, minus = tables()
    vmem = pl.BlockSpec(memory_space=pltpu.VMEM)
    smem = pl.BlockSpec(memory_space=pltpu.SMEM)
    anywhere = pl.BlockSpec(memory_space=pl.ANY)
    dma = pltpu.SemaphoreType.DMA
    return pl.pallas_call(
        kernel,
        out_shape=pltpu.VMEM(orbitals.shape, F32),
        in_specs=[smem, smem, anywhere, vmem, vmem],
        out_specs=vmem,
        scratch_shapes=[
            pltpu.VMEM((CHUNKS, 6, SLAB, LANES), BF),
            pltpu.VMEM((CHUNKS, 4, 2, SLAB, LANES), BF),
            pltpu.VMEM((TILES, 8 * GRID, GRID), F32),
            pltpu.VMEM((TILES, 8 * GRID, GRID), F32),
            pltpu.VMEM((GRID, GRID, GRID), F32),
            pltpu.VMEM((CHUNKS, 8, SLAB, LANES), BF),
            pltpu.VMEM((CHUNKS, 2, 2, SLAB, LANES), BF),
            pltpu.VMEM((CHUNKS, 2, SLAB, LANES), BF),
            pltpu.VMEM((8, GRID), F32),
            pltpu.VMEM((8, GRID), F32),
            dma((1,)),
            dma((11,)),
            dma((4, CHUNKS)),
            dma((9,)),
            dma((5, CHUNKS)),
            dma((2,)),
        ],
        compiler_params=pltpu.CompilerParams(
            collective_id=0, has_side_effects=True, vmem_limit_bytes=58 * 1024 * 1024
        ),
        name="exchange",
    )(occupation, pair_keep, orbitals, jnp.asarray(plus), jnp.asarray(minus))


def solution(mesh):
    in_specs = (P("band", "grid", None), P("band"), P("band", None, None))
    return jax.shard_map(
        body, mesh=mesh, in_specs=in_specs, out_specs=P("band", "grid", None), check_vma=False
    )
```

```python
import functools
import math

import jax
import jax.numpy as jnp
import numpy as np
from jax import lax
from jax.experimental import pallas as pl
from jax.experimental.pallas import tpu as pltpu
from jax.sharding import PartitionSpec as P

GRID = 128
SLAB = 32
BLOCKS = 32
HALF_RING = 16
WIDTH = 64.0
CHUNKS = 16
LANES = GRID * GRID // CHUNKS
PAIRS = LANES // (2 * GRID)
TILES = GRID // 8
IN_LAGS = (4, 6, 10)
OUT_LAGS = (3, 3, 4, 6)
THIRDS = CHUNKS // 3
BF = jnp.bfloat16
F32 = jnp.float32
MESH = pl.DeviceIdType.MESH


def tables():
    index = np.arange(GRID)
    angle = (index[:, None] * index[None, :] % GRID) * (2.0 * math.pi / GRID)
    cosine, sine = np.cos(angle), np.sin(angle)
    forward = np.block([[cosine, -sine], [sine, cosine]])
    return tuple(np.asarray(t, np.float32).astype(BF) for t in (forward, forward.T))


def dot(left, right):
    return jnp.dot(left, right, preferred_element_type=F32)


def regroup(value):
    n = GRID
    top = jnp.concatenate([value[:n, :n], value[n:, :n]], 1)
    low = jnp.concatenate([value[:n, n:], value[n:, n:]], 1)
    return jnp.concatenate([top, low], 0)


def kernel(
    occ, keep, orbitals, plus, minus, out,
    lead, own, real, imag, factor, sums_in, core_in, chip_in, note_out, note_in,
    load_sem, send_a, recv_a, send_b, recv_b, note_sem,
):
    c, g = lax.axis_index("band"), lax.axis_index("grid")
    p, k = lax.div(g, 2), lax.rem(g, 2)
    spot = lax.rem(c, HALF_RING)
    z = lax.rem(c, 4)

    def block(step):
        return lax.rem(c + BLOCKS + step, BLOCKS)

    def flag(condition):
        return jnp.where(condition, 1, 0)

    cross = {
        step: flag(spot >= HALF_RING - step) if step > 0 else flag(spot < -step)
        for step in (1, 2, 3, -1, -2, -3)
    }

    def flip(value, bit):
        return value + bit - 2 * value * bit

    def slot_of(quarter):
        return 2 * flip(quarter // 2, p) + flip(quarter % 2, k)

    def remote(source, target, sends, receives, kind, sort, n, device):
        return pltpu.make_async_remote_copy(
            src_ref=source,
            dst_ref=target,
            send_sem=sends.at[kind],
            recv_sem=receives.at[sort, n],
            device_id=device,
            device_id_type=MESH,
        )

    other_core = (c, 2 * p + 1 - k)
    other_chip = (c, 2 * (1 - p) + k)

    def part(n):
        return pl.ds(pl.multiple_of(n * LANES, LANES), LANES)

    def third(n):
        return (lax.rem(n, 2) == 0) & (n < 2 * THIRDS)

    def each(count, step):
        def run(n, carry):
            step(n)
            return carry

        lax.fori_loop(0, count, run, 0)

    barrier = pltpu.get_barrier_semaphore()

    def greet(band, grid):
        pl.semaphore_signal(barrier, inc=1, device_id=(band, grid), device_id_type=MESH)

    for step in (1, -1):

        @pl.when(cross[step] == 1)
        def _(step=step):
            for core in (0, 1):
                greet(block(step), 2 * (1 - p) + core)

    for step in (3, -3, 1, -1, 2, -2):
        for core in (0, 1):
            greet(block(step), 2 * (flip(p, cross[step]) if abs(step) == 3 else p) + core)
    greet(*other_core)
    greet(*other_chip)

    fetch = pltpu.make_async_copy(orbitals, out, load_sem.at[0])
    fetch.start()

    def clear(n):
        @pl.when((k == 0) | third(n))
        def _():
            sums_in[n, 2] = jnp.zeros((SLAB, LANES), BF)

    each(CHUNKS, clear)
    note_out[...] = jnp.zeros((8, GRID), F32) + occ[p]
    fetch.wait()
    own[0, 0] = out[:, :, part(0)].astype(BF)
    pl.semaphore_wait(barrier, 14 + 2 * (cross[1] + cross[-1]))

    note = pltpu.make_async_remote_copy(
        src_ref=note_out,
        dst_ref=note_in,
        send_sem=note_sem.at[0],
        recv_sem=note_sem.at[1],
        device_id=(lax.rem(c + 1 + k, BLOCKS), g),
        device_id_type=MESH,
    )
    note.start()

    def in_bands(n):
        mine = own.at[n, 0]
        return (
            remote(mine, own.at[n, 2], send_a, recv_a, 0, 0, n, other_chip),
            remote(mine, own.at[n, 1], send_a, recv_a, 1, 1, n, other_core),
        )

    def in_core(n):
        return remote(own.at[n, 2], own.at[n, 3], send_a, recv_a, 4, 1, n, other_core)

    def in_one(n, far):
        chip = flip(p, cross[1])
        return remote(
            own.at[n, 2 * flip(far, cross[1]), chip],
            lead.at[n, k + 2 * far],
            send_a,
            recv_a,
            2 + far,
            2 - far,
            n,
            (block(1), 2 * chip),
        )

    def in_two(n, far):
        chip = flip(p, cross[2])
        direct = z == 1
        step = jnp.where(direct, 2, jnp.where(z == 0, 3, -1))
        device = jnp.where(direct, 2 * chip + 1, g)
        return remote(
            own.at[n, 2 * flip(far, cross[2]), chip],
            lead.at[n, jnp.where(direct, 1 - k + 2 * far, 4 + far)],
            send_a,
            recv_a,
            5 + far,
            jnp.where(direct, 2 - far, 3),
            n,
            (block(step), device),
        )

    in_between = z != 0

    def in_pass(n, far):
        chip = flip(p, flag((spot == HALF_RING - 3) | (spot == HALF_RING - 2)))
        return remote(
            lead.at[n, 4 + far],
            lead.at[n, 1 - k + 2 * far],
            send_a,
            recv_a,
            7 + far,
            2 - far,
            n,
            (block(jnp.where(z == 3, -1, 3)), 2 * chip + 1),
        )

    def in_share(n, slot):
        return remote(
            lead.at[n, slot],
            lead.at[n, 1 - slot],
            send_a,
            recv_a,
            9 + slot,
            2,
            n,
            (block(1), 2 * p + 1),
        )

    def in_leads(n, second):
        in_one(n, flip(second, cross[1])).start()
        far = flip(second, cross[2])

        @pl.when((far == 1) | ((k == 1) & jnp.logical_not(third(n))))
        def _():
            in_two(n, far).start()

    def sent(ref, sends, kind):
        pltpu.make_async_remote_copy(
            src_ref=ref,
            dst_ref=ref,
            send_sem=sends.at[kind],
            recv_sem=note_sem.at[1],
            device_id=other_core,
            device_id_type=MESH,
        ).wait_send()

    def arrived_a(ref, sort, n):
        remote(ref, ref, send_a, recv_a, 0, sort, n, other_core).wait_recv()

    def make_factor(n):
        shape = (GRID, GRID)
        rows = lax.broadcasted_iota(jnp.int32, shape, 0)
        columns = lax.broadcasted_iota(jnp.int32, shape, 1)

        def squared(index):
            freq = jnp.where(index >= GRID // 2, index - GRID, index).astype(F32)
            return freq * freq

        base = squared(rows) + squared(columns)

        def plane(i, carry):
            kx = n * (GRID // CHUNKS) + i
            q = (base + squared(jnp.full(shape, kx, jnp.int32))) * (1.0 / WIDTH)
            safe = jnp.where(q > 0, q, 1.0)
            ratio = jnp.where(q > 0, (1.0 - jnp.exp(-safe)) / safe, 1.0)
            factor[kx] = ratio * (4.0 / GRID**3)
            return carry

        lax.fori_loop(0, GRID // CHUNKS, plane, 0)

    def rows_of(y):
        return pl.ds(pl.multiple_of(y * 8, 8), 8)

    def forward(n):
        for pair in range(PAIRS):
            lanes = slice(pair * 2 * GRID, (pair + 1) * 2 * GRID)
            slots = [slot_of(quarter) for quarter in range(4)]
            first = jnp.concatenate([lead[n, s, :, lanes] for s in slots], 0)
            parts = [
                first * jnp.concatenate([own[n, s, j, :, lanes] for s in slots], 0)
                for j in range(2)
            ]
            mixed = regroup(dot(minus[...], jnp.concatenate(parts, 0)).astype(BF))
            result = dot(mixed, plus[...])
            for half in range(2):
                rows = rows_of(n * 2 * PAIRS + 2 * pair + half)
                for t in range(TILES):
                    at = half * GRID + t * 8
                    real[t, rows, :] = result[at : at + 8, :GRID]
                    imag[t, rows, :] = result[at : at + 8, GRID:]

    def in_step(n, carry):
        @pl.when(n < CHUNKS)
        def _():
            for copy in in_bands(n):
                copy.start()
            in_leads(n, 0)
            later = jnp.minimum(n + 1, CHUNKS - 1)

            @pl.when(later > n)
            def _():
                own[later, 0] = out[:, :, part(later)].astype(BF)

            make_factor(n)

        @pl.when((n >= IN_LAGS[0]) & (n < CHUNKS + IN_LAGS[0]))
        def _():
            m = n - IN_LAGS[0]
            arrived_a(own.at[m, 2], 0, m)
            in_leads(m, 1)
            in_core(m).start()

        @pl.when((n >= IN_LAGS[1]) & (n < CHUNKS + IN_LAGS[1]))
        def _():
            m = n - IN_LAGS[1]

            @pl.when(in_between)
            def _():
                both = (k == 1) & jnp.logical_not(third(m))

                @pl.when(both)
                def _():
                    arrived_a(lead.at[m, 4:6], 3, m)
                    in_pass(m, 0).start()

                @pl.when(jnp.logical_not(both))
                def _():
                    arrived_a(lead.at[m, 5], 3, m)

                in_pass(m, 1).start()

            @pl.when(k == 0)
            def _():
                arrived_a(lead.at[m, 0:2], 2, m)
                in_share(m, 0).start()

                @pl.when(third(m))
                def _():
                    in_share(m, 1).start()

        @pl.when(n >= IN_LAGS[2])
        def _():
            m = n - IN_LAGS[2]

            @pl.when(k == 1)
            def _():
                arrived_a(lead.at[m, 0:2], 2, m)

            arrived_a(own.at[m, 0:3], 1, m)
            forward(m)

        return carry

    lax.fori_loop(0, CHUNKS + IN_LAGS[2], in_step, 0)

    def middle(step):
        for t in (8 * step + i for i in range(8)):
            for pair in range(4):
                pick = [pl.ds(2 * pair + half, GRID, stride=8) for half in range(2)]
                packed = jnp.concatenate(
                    [jnp.concatenate([w[t, r, :] for r in pick], 1) for w in (real, imag)], 0
                ).astype(BF)
                scale = jnp.concatenate(
                    [factor[t * 8 + 2 * pair], factor[t * 8 + 2 * pair + 1]], 1
                )
                scale = jnp.concatenate([scale, scale], 0)
                field = (dot(minus[...], packed) * scale).astype(BF)
                result = dot(plus[...], field)
                for half in range(2):
                    at = slice(half * GRID, (half + 1) * GRID)
                    real[t, pick[half], :] = result[:GRID, at]
                    imag[t, pick[half], :] = result[GRID:, at]

    each(TILES // 8, middle)

    one, some, rest = lead.at[:, 0], lead.at[:THIRDS, 0], lead.at[THIRDS:, 0]
    for kind, ref in enumerate((own.at[:, 0], own.at[:, 0], one, one, own.at[:, 2])):
        sent(ref, send_a, kind)
    sent(one, send_a, 6)

    @pl.when(k == 1)
    def _():
        sent(rest, send_a, 5)

    @pl.when(k == 0)
    def _():
        sent(one, send_a, 9)
        sent(some, send_a, 10)

    @pl.when(in_between)
    def _():
        sent(one, send_a, 8)

        @pl.when(k == 1)
        def _():
            sent(rest, send_a, 7)

    note.wait()
    kept = [keep[j, k, p].astype(F32) for j in range(2)]
    own0, own1 = (-(occ[j] * kept[j]) for j in range(2))
    amount = jnp.concatenate([note_in[0:1, :]] * 2, 1)
    lead0, lead1 = (-(amount * kept[j]) for j in range(2))

    def inverse(n):
        for pair in range(PAIRS):
            lanes = slice(pair * 2 * GRID, (pair + 1) * 2 * GRID)

            def field(w):
                halves = []
                for half in range(2):
                    rows = rows_of(n * 2 * PAIRS + 2 * pair + half)
                    halves.append(jnp.concatenate([w[t, rows, :] for t in range(TILES)], 0))
                return jnp.concatenate(halves, 1)

            packed = jnp.concatenate([field(real), field(imag)], 0).astype(BF)
            mixed = regroup(dot(plus[...], packed).astype(BF))
            potential = dot(mixed, minus[...])
            v0 = jnp.concatenate([potential[:GRID, :GRID], potential[GRID:, :GRID]], 1)
            v1 = jnp.concatenate([potential[:GRID, GRID:], potential[GRID:, GRID:]], 1)
            for quarter in range(4):
                s = slot_of(quarter)
                rows = slice(quarter * SLAB, (quarter + 1) * SLAB)
                x0, x1 = v0[rows], v1[rows]
                a = lead[n, s, :, lanes].astype(F32)
                b0 = own[n, s, 0, :, lanes].astype(F32)
                b1 = own[n, s, 1, :, lanes].astype(F32)
                lead[n, s, :, lanes] = ((own0 * x0) * b0 + (own1 * x1) * b1).astype(BF)
                own[n, s, 0, :, lanes] = ((lead0 * x0) * a).astype(BF)
                own[n, s, 1, :, lanes] = ((lead1 * x1) * a).astype(BF)

    def out_core(n):
        return (
            remote(own.at[n, 1], core_in.at[n, 0], send_b, recv_b, 0, 1, n, other_core),
            remote(own.at[n, 3], core_in.at[n, 1], send_b, recv_b, 1, 0, n, other_core),
        )

    def out_one(n, slot):
        far = slot // 2
        return remote(
            lead.at[n, slot],
            sums_in.at[n, far],
            send_b,
            recv_b,
            2 + slot,
            1 - flip(far, cross[-1]),
            n,
            (block(-1), 2 * flip(p, cross[-1]) + slot % 2),
        )

    def out_two(n, slot):
        far = slot // 2
        core = 1 - slot % 2
        direct = z == 2
        step = jnp.where(direct, -2, jnp.where(z == 3, -3, 1))
        chip = jnp.where(direct, flip(p, cross[-2]), p)
        index = far + jnp.where(direct, 2, 4)
        return remote(
            lead.at[n, slot],
            sums_in.at[n, index],
            send_b,
            recv_b,
            2 + slot,
            jnp.where(direct, 2 - 2 * far, 3 + far),
            n,
            (block(step), 2 * chip + core),
        )

    out_between = z != 3

    def out_pass(n, far):
        chip = flip(p, flag((spot == 1) | (spot == 2)))
        return remote(
            sums_in.at[n, 4 + far],
            sums_in.at[n, 2 + far],
            send_b,
            recv_b,
            6 + far,
            2 - 2 * far,
            n,
            (block(jnp.where(z == 0, 1, -3)), 2 * chip + k),
        )

    def out_share(n, slot):
        return remote(
            lead.at[n, slot],
            sums_in.at[n, 7 - slot],
            send_b,
            recv_b,
            2 + slot,
            3 - slot,
            n,
            (block(-1), 2 * p),
        )

    def out_chip(n):
        return remote(own.at[n, 2], chip_in.at[n], send_b, recv_b, 8, 1, n, other_chip)

    def arrived_b(ref, sort, n):
        remote(ref, ref, send_b, recv_b, 0, sort, n, other_core).wait_recv()

    bands = [flip(p, cross[1]), flip(p, cross[2])]
    masks = [[flag(b == band).astype(F32) for b in bands] for band in range(2)]

    def lead_sums(m, far, band):
        first = sums_in[m, flip(far, cross[1])].astype(F32)
        second = sums_in[m, 2 + flip(far, cross[2])].astype(F32)
        return masks[band][0] * first + masks[band][1] * second

    def out_step(n, carry):
        @pl.when(n < CHUNKS)
        def _():
            inverse(n)

            @pl.when(k == 0)
            def _():
                out_one(n, 2).start()
                out_one(n, 3).start()

                @pl.when(jnp.logical_not(third(n)))
                def _():
                    out_one(n, 1).start()

            @pl.when(k == 1)
            def _():
                out_share(n, 1).start()
                out_two(n, 2).start()
                out_two(n, 3).start()

                @pl.when(third(n))
                def _():
                    out_share(n, 0).start()

                @pl.when(jnp.logical_not(third(n)))
                def _():
                    out_two(n, 0).start()

            for copy in out_core(n):
                copy.start()

        @pl.when((n >= OUT_LAGS[0]) & (n < CHUNKS + OUT_LAGS[0]))
        def _():
            m = n - OUT_LAGS[0]

            @pl.when(out_between)
            def _():
                arrived_b(sums_in.at[m, 5], 4, m)
                out_pass(m, 1).start()

                @pl.when((k == 1) & jnp.logical_not(third(m)))
                def _():
                    arrived_b(sums_in.at[m, 4], 3, m)
                    out_pass(m, 0).start()

        @pl.when((n >= OUT_LAGS[1]) & (n < CHUNKS + OUT_LAGS[1]))
        def _():
            m = n - OUT_LAGS[1]

            @pl.when(k == 0)
            def _():
                arrived_b(sums_in.at[m, 6], 2, m)
                total = lead[m, 0].astype(F32) + sums_in[m, 6].astype(F32)
                lead[m, 0] = total.astype(BF)
                out_one(m, 0).start()

                @pl.when(third(m))
                def _():
                    arrived_b(sums_in.at[m, 7], 3, m)
                    total = lead[m, 1].astype(F32) + sums_in[m, 7].astype(F32)
                    lead[m, 1] = total.astype(BF)
                    out_one(m, 1).start()

        @pl.when((n >= OUT_LAGS[2]) & (n < CHUNKS + OUT_LAGS[2]))
        def _():
            m = n - OUT_LAGS[2]
            arrived_b(sums_in.at[m, 0:4], 0, m)

            @pl.when((k == 1) & jnp.logical_not(third(m)))
            def _():
                arrived_b(sums_in.at[m, 2], 2, m)

            for band in range(2):
                total = own[m, 2, band].astype(F32) + core_in[m, 1, band].astype(F32)
                own[m, 2, band] = (total + lead_sums(m, 1, band)).astype(BF)
            out_chip(m).start()

        @pl.when(n >= OUT_LAGS[3])
        def _():
            m = n - OUT_LAGS[3]
            arrived_b(sums_in.at[m, 0:5], 1, m)
            for band in range(2):
                total = own[m, 0, band].astype(F32) + core_in[m, 0, band].astype(F32)
                out[band, :, part(m)] = (
                    total + chip_in[m, band].astype(F32) + lead_sums(m, 0, band)
                )

        return carry

    lax.fori_loop(0, CHUNKS + OUT_LAGS[3], out_step, 0)

    for kind, ref in enumerate((own.at[:, 0],) * 2 + (one,) * 4):
        sent(ref, send_b, kind)

    @pl.when(out_between)
    def _():
        sent(one, send_b, 7)

        @pl.when(k == 1)
        def _():
            sent(rest, send_b, 6)

    sent(own.at[:, 2], send_b, 8)


def body(orbitals, occupation, pair_keep):
    plus, minus = tables()
    vmem = pl.BlockSpec(memory_space=pltpu.VMEM)
    smem = pl.BlockSpec(memory_space=pltpu.SMEM)
    anywhere = pl.BlockSpec(memory_space=pl.ANY)
    dma = pltpu.SemaphoreType.DMA
    return pl.pallas_call(
        kernel,
        out_shape=pltpu.VMEM(orbitals.shape, F32),
        in_specs=[smem, smem, anywhere, vmem, vmem],
        out_specs=vmem,
        scratch_shapes=[
            pltpu.VMEM((CHUNKS, 6, SLAB, LANES), BF),
            pltpu.VMEM((CHUNKS, 4, 2, SLAB, LANES), BF),
            pltpu.VMEM((TILES, 8 * GRID + 8, GRID), F32),
            pltpu.VMEM((TILES, 8 * GRID + 8, GRID), F32),
            pltpu.VMEM((GRID, GRID, GRID), F32),
            pltpu.VMEM((CHUNKS, 8, SLAB, LANES), BF),
            pltpu.VMEM((CHUNKS, 2, 2, SLAB, LANES), BF),
            pltpu.VMEM((CHUNKS, 2, SLAB, LANES), BF),
            pltpu.VMEM((8, GRID), F32),
            pltpu.VMEM((8, GRID), F32),
            dma((1,)),
            dma((11,)),
            dma((4, CHUNKS)),
            dma((9,)),
            dma((5, CHUNKS)),
            dma((2,)),
        ],
        compiler_params=pltpu.CompilerParams(
            collective_id=0, has_side_effects=True, vmem_limit_bytes=58 * 1024 * 1024
        ),
        name="exchange",
    )(occupation, pair_keep, orbitals, jnp.asarray(plus), jnp.asarray(minus))


def solution(mesh):
    in_specs = (P("band", "grid", None), P("band"), P("band", None, None))
    return jax.shard_map(
        body, mesh=mesh, in_specs=in_specs, out_specs=P("band", "grid", None), check_vma=False
    )
```
